128 devices in a mesh: dp: 4 (over x), vocab: 32 (over y, z, core).
Axes of the slice: x: 4, y: 4, z: 4, core: 2. Of those that a mesh axis runs over, the one named last changes fastest.
Arguments:
- hidden: bfloat16 [2048, 4096], P('dp', 'vocab'), may hold values from -100 to 100
- head_weight: bfloat16 [4096, 75968], P(None, 'vocab'), may hold values from -1 to 1
- teacher_logits: bfloat16 [2048, 75968], P(('dp', 'vocab')), may hold values from -400 to 400
- row_weight: float32 [2048], P('dp'), may hold values from 9496 to 151936
Outputs:
- kl_rows: float32 [2048], P('dp')
- grad_hidden: bfloat16 [2048, 4096], P('dp', 'vocab')
- grad_head: bfloat16 [4096, 75968], P('dp', 'vocab')
The draws below stay inside these ranges and needn't reach their ends.
All inputs are finite; a program needn't handle non-finite values.
Results may differ from the reference program's by a relative error of at most 0.017.
Values may be sent and summed in bfloat16 or wider, within the bound.
No kernel may reach another device: no remote copies, remote signals or barrier semaphores. Data moves between devices by JAX's collectives and lax.ppermute only.
A program may use at most 192 MiB of HBM per device.

```python
import math
import jax
import jax.numpy as jnp
from jax import lax

D = 4096
V = 75968
TOKENS = 2048
N_DP = 4


def draw_head_weight(key, part):
    key = jax.random.fold_in(key, 1)
    base = jnp.clip(jax.random.normal(key, (D, V), jnp.float32), -5.0, 5.0) / D ** 0.5
    return base.astype(jnp.bfloat16)


def draw_hidden(key, part):
    key = jax.random.fold_in(key, 2)
    base = jnp.clip(jax.random.normal(key, (TOKENS, D), jnp.float32), -4.0, 4.0) * 0.3
    return base.astype(jnp.bfloat16)


def draw_teacher_logits(key, part):
    key = jax.random.fold_in(key, 3)
    key_base, key_scale = jax.random.split(key)
    ramp = math.log(3.0) * jnp.arange(V, dtype=jnp.float32) / V
    row_sigma = 0.25 * jnp.exp(jax.random.uniform(key_scale, (TOKENS, 1), jnp.float32, 0.0, math.log(3.0)))
    base = jnp.clip(jax.random.normal(key_base, (TOKENS, V), jnp.float32), -6.0, 6.0) * row_sigma
    base = base + ramp[None, :]
    return base.astype(jnp.bfloat16)


def steps_of(key, dims, pieces, low, largest):
    def one(position, blocks):
        steps = jax.random.uniform(jax.random.fold_in(jax.random.fold_in(key, 6), position), (blocks,), jnp.float32, low / len(pieces), largest / len(pieces))
        return jnp.repeat(jnp.exp(steps), dims[position] // blocks).reshape((-1,) + (1,) * (len(dims) - position - 1))

    gain = one(*pieces[0])
    for cut in pieces[1:]:
        gain = gain * one(*cut)
    return gain


def setup_inputs(seed: int = 0) -> dict:
    arg_keys = jax.random.split(jax.random.key(seed), 5)
    return {
        "hidden": draw_hidden(jax.random.fold_in(arg_keys[4], 71), 0),
        "head_weight": draw_head_weight(jax.random.fold_in(arg_keys[4], 71), 0),
        "teacher_logits": draw_teacher_logits(jax.random.fold_in(arg_keys[4], 71), 0),
        "row_weight": jnp.clip(jnp.exp(math.log(151936.0) - 2.7725887 * jax.random.uniform(arg_keys[3], (TOKENS,), jnp.float32) ** steps_of(arg_keys[3], (TOKENS,), ((0, 4),), -0.2, 0.2)), 9496.0, 151936.0),
    }


def reference(hidden, head_weight, teacher_logits, row_weight):
    group_size = TOKENS // N_DP
    kl_parts = []
    grad_parts = []
    head_total = jnp.zeros((D, V), jnp.float32)
    for group_index in range(N_DP):
        lower = group_index * group_size
        states = hidden[lower:lower + group_size]
        student = jnp.dot(states, head_weight, preferred_element_type=jnp.float32)
        teacher = teacher_logits[lower:lower + group_size].astype(jnp.float32)
        student_peak = jnp.max(student, axis=1)
        teacher_peak = jnp.max(teacher, axis=1)
        student_exp = jnp.exp(student - student_peak[:, None])
        teacher_exp = jnp.exp(teacher - teacher_peak[:, None])
        student_total = jnp.sum(student_exp, axis=1)
        teacher_total = jnp.sum(teacher_exp, axis=1)
        teacher_cross = jnp.sum(teacher_exp * (teacher - student), axis=1)
        kl_parts.append(teacher_cross / teacher_total - teacher_peak - jnp.log(teacher_total)
                        + student_peak + jnp.log(student_total))
        weights = row_weight[lower:lower + group_size]
        grad_logits = (weights[:, None] * (student_exp / student_total[:, None]
                                           - teacher_exp / teacher_total[:, None])).astype(jnp.bfloat16)
        grad_parts.append(jnp.dot(grad_logits, head_weight.T, preferred_element_type=jnp.float32).astype(jnp.bfloat16))
        partial_head = lax.dot_general(states, grad_logits, (((0,), (0,)), ((), ())),
                                       preferred_element_type=jnp.float32)
        rounded = lax.optimization_barrier(partial_head.astype(jnp.bfloat16))
        head_total = head_total + rounded.astype(jnp.float32)
    return (jnp.concatenate(kl_parts, axis=0), jnp.concatenate(grad_parts, axis=0),
            head_total.astype(jnp.bfloat16))
```

```python
import functools

import jax
import jax.numpy as jnp
from jax import lax
from jax.experimental import pallas as pl
from jax.experimental.pallas import tpu as pltpu
from jax.sharding import Mesh
from jax.sharding import PartitionSpec as P

F32, BF16 = jnp.float32, jnp.bfloat16
V = ("y", "z", "c")
NV = 32
VL = 2374
VP = 2432
VB = 608
NB = VP // VB
KK = 10
TC = 256
NCH = 2
D = 4096
DX = 1024
LOW = -1e30
MIB = 1 << 20


def call(body, **kw):
    flops, nbytes = kw.pop("cost")
    limit = kw.pop("limit", 60)
    return pl.pallas_call(
        body,
        compiler_params=pltpu.CompilerParams(vmem_limit_bytes=limit * MIB),
        cost_estimate=pl.CostEstimate(flops=flops // 100, bytes_accessed=nbytes // 100, transcendentals=0),
        **kw,
    )


def whole(shape):
    return pl.BlockSpec(shape, lambda *_: (0,) * len(shape))


def prep_body(t_ref, *outs):
    for i in range(NV):
        lo = VL * i
        for k in range(KK):
            pair = []
            for n in (2 * k, 2 * k + 1):
                start = lo + n * 128
                if n * 128 >= VL:
                    pair.append(jnp.zeros((16, 128), F32))
                    continue
                if start + 128 <= NV * VL:
                    pair.append(t_ref[:, start : start + 128].astype(F32))
                else:
                    last = NV * VL - 128
                    tile = t_ref[:, last : last + 128].astype(F32)
                    pair.append(pltpu.roll(tile, 128 - (start - last), axis=1))
            for c in range(NCH):
                rows = slice(8 * c, 8 * c + 8)
                outs[c][i, k] = jnp.concatenate([pair[0][rows], pair[1][rows]], axis=0).astype(BF16)


def prep(teacher):
    shape = (NV, KK, 16, 128)
    return call(
        prep_body,
        out_shape=[jax.ShapeDtypeStruct(shape, BF16)] * NCH,
        grid=(1,),
        in_specs=[whole(teacher.shape)],
        out_specs=[whole(shape)] * NCH,
        cost=(0, 5 << 20),
    )(teacher)


def student_body(first, pos, w_ref, own_ref, sib_ref, *refs):
    s_ref, m_ref, h_ref = refs[-3:]
    step = pl.program_id(0)

    @pl.when(step == 0)
    def _():
        for a in range(4):
            for b in range(4):
                j = (((pos[1] + 4 - a) % 4) * 4 + (pos[2] + 4 - b) % 4) * 2
                for ref, c in ((own_ref, pos[3]), (sib_ref, 1 - pos[3])):
                    h_ref[:, pl.ds(pl.multiple_of((j + c) * 128, 128), 128)] = ref[a, b]
        m_ref[...] = refs[0][...] if first else jnp.full_like(m_ref, LOW)

    s = lax.dot_general(w_ref[...], h_ref[...], (((1,), (1,)), ((), ())), preferred_element_type=F32)
    rows = (first + step) * VB + lax.broadcasted_iota(jnp.int32, s.shape, 0)
    s = jnp.where(rows < VL, s, LOW)
    s_ref[...] = s
    m_ref[...] = jnp.maximum(m_ref[...], jnp.max(s.reshape(VB // 8, 8, TC), axis=0))


def student_chunk(pos, wt, own, sib, first=0, steps=NB, prior=()):
    specs = [
        pl.BlockSpec((VB, D), lambda i, p: (first + i, 0)),
        whole((4, 4, TC, 128)),
        whole((4, 4, TC, 128)),
    ]
    kw = {}
    if prior:
        specs += [whole((8, TC)), pl.BlockSpec(memory_space=pl.ANY)]
        kw["input_output_aliases"] = {5: 0}
    return call(
        functools.partial(student_body, first),
        out_shape=[jax.ShapeDtypeStruct((VP, TC), F32), jax.ShapeDtypeStruct((8, TC), F32)],
        grid_spec=pltpu.PrefetchScalarGridSpec(
            num_scalar_prefetch=1,
            grid=(steps,),
            in_specs=specs,
            out_specs=[pl.BlockSpec((VB, TC), lambda i, p: (first + i, 0)), whole((8, TC))],
            scratch_shapes=[pltpu.VMEM((TC, D), BF16)],
        ),
        cost=(2 * VP * TC * D, VP * D * 2 + VP * TC * 4 + 4 * MIB),
        **kw,
    )(pos, wt, own, sib, *prior[::-1])


def stats_body(s_ref, m_ref, t_ref, tt_ref, out_ref, x_ref):
    peak = jnp.full((8, TC), LOW, F32)
    for n in range(VP // 128):
        half = t_ref[:, n // 2].astype(F32)[:, 8 * (n % 2) : 8 * (n % 2) + 8, :]
        x = half.reshape(TC, 128).T
        if (n + 1) * 128 > VL:
            rows = n * 128 + lax.broadcasted_iota(jnp.int32, x.shape, 0)
            x = jnp.where(rows < VL, x, LOW)
        x_ref[n * 128 : (n + 1) * 128, :] = x
        tt_ref[n * 128 : (n + 1) * 128, :] = x.astype(BF16)
        peak = jnp.maximum(peak, jnp.max(x.reshape(16, 8, TC), axis=0))
    t_peak = jnp.max(peak, axis=0, keepdims=True)
    s_peak = jnp.max(m_ref[...], axis=0, keepdims=True)
    zero = jnp.zeros((8, TC), F32)

    def add(n, sums):
        s_sum, t_sum, cross = sums
        rows = pl.ds(n * 64, 64)
        s, t = s_ref[rows, :], x_ref[rows, :]
        es, et = jnp.exp(s - s_peak), jnp.exp(t - t_peak)
        fold = lambda v: jnp.sum(v.reshape(8, 8, TC), axis=0)
        return s_sum + fold(es), t_sum + fold(et), cross + fold(et * (t - s))

    sums = lax.fori_loop(0, VP // 64, add, (zero, zero, zero))
    sums = [jnp.sum(v, axis=0, keepdims=True) for v in sums]
    row = lax.broadcasted_iota(jnp.int32, (8, TC), 0)
    out = jnp.zeros((8, TC), F32)
    for n, v in enumerate([s_peak, t_peak] + sums):
        out = jnp.where(row == n, v, out)
    out_ref[...] = out


def stats_chunk(s, m, t):
    return call(
        stats_body,
        out_shape=[jax.ShapeDtypeStruct((VP, TC), BF16), jax.ShapeDtypeStruct((8, TC), F32)],
        grid=(1,),
        in_specs=[whole((VP, TC)), whole((8, TC)), whole((NV, KK, 16, 128))],
        out_specs=[whole((VP, TC)), whole((8, TC))],
        scratch_shapes=[pltpu.VMEM((VP, TC), F32)],
        cost=(VP * TC * 40, 6 * MIB),
    )(s, m, t)


def merged(refs):
    if len(refs) == 1:
        v = refs[0][...]
        s_peak, t_peak = jnp.max(v[:, 0:1, :], axis=0), jnp.max(v[:, 1:2, :], axis=0)
        se, te = jnp.exp(v[:, 0:1, :] - s_peak[None]), jnp.exp(v[:, 1:2, :] - t_peak[None])
        total = lambda scale, n: jnp.sum(scale * v[:, n : n + 1, :], axis=0)
        return s_peak, t_peak, total(se, 2), total(te, 3), total(te, 4)
    get = lambda n: [r[n : n + 1, :] for r in refs]
    s_peak, t_peak = functools.reduce(jnp.maximum, get(0)), functools.reduce(jnp.maximum, get(1))
    se = [jnp.exp(p - s_peak) for p in get(0)]
    te = [jnp.exp(p - t_peak) for p in get(1)]
    total = lambda scales, n: sum(a * b for a, b in zip(scales, get(n)))
    return s_peak, t_peak, total(se, 2), total(te, 3), total(te, 4)


def merge_body(*refs):
    refs[-1][...] = jnp.zeros((8, TC), F32)
    for n, v in enumerate(merged(refs[:-1])):
        refs[-1][n : n + 1, :] = v


def merge(parts):
    shape = (8, TC)
    return call(
        merge_body,
        out_shape=jax.ShapeDtypeStruct(shape, F32),
        grid=(1,),
        in_specs=[whole(shape)] * len(parts),
        out_specs=whole(shape),
        cost=(0, 8192),
    )(*parts)


def grad_body(*refs):
    w_ref, s_ref, t_ref, *g_refs, kl_ref, c_ref = refs[-7:]

    @pl.when(pl.program_id(0) == 0)
    def _():
        s_peak, t_peak, s_tot, t_tot, cross = merged(refs[:-7])
        kl_ref[...] = cross / t_tot - t_peak - jnp.log(t_tot) + s_peak + jnp.log(s_tot)
        c_ref[0:1, :] = s_peak
        c_ref[1:2, :] = t_peak
        c_ref[2:3, :] = w_ref[...] / s_tot
        c_ref[3:4, :] = w_ref[...] / t_tot

    es = jnp.exp(s_ref[...] - c_ref[0:1, :]) * c_ref[2:3, :]
    et = jnp.exp(t_ref[...].astype(F32) - c_ref[1:2, :]) * c_ref[3:4, :]
    g = (es - et).astype(BF16)
    for half in range(2):

        @pl.when(pl.program_id(0) // (NB // 2) == half)
        def _():
            g_refs[half][...] = g


def grad_chunk(shares, w, s, t):
    block = pl.BlockSpec((VB, TC), lambda i: (i, 0))
    return call(
        grad_body,
        out_shape=[jax.ShapeDtypeStruct((VP // 2, TC), BF16)] * 2 + [jax.ShapeDtypeStruct((1, TC), F32)],
        grid=(NB,),
        in_specs=[whole(x.shape) for x in shares] + [whole((1, TC)), block, block],
        out_specs=[
            pl.BlockSpec((VB, TC), lambda i: (jnp.minimum(i, NB // 2 - 1), 0)),
            pl.BlockSpec((VB, TC), lambda i: (jnp.maximum(i - NB // 2, 0), 0)),
            whole((1, TC)),
        ],
        scratch_shapes=[pltpu.VMEM((8, TC), F32)],
        cost=(VP * TC * 30, 6 * MIB),
    )(*shares, w, s, t)


def hidden_body(pos, g0_ref, g1_ref, w_ref, mine_ref, other_ref, gt_ref):
    @pl.when(pl.program_id(0) == 0)
    def _():
        half = VP // 2
        for lo in range(0, VP, 128):
            if lo + 128 <= half:
                x = g0_ref[lo : lo + 128, :]
            elif lo >= half:
                x = g1_ref[lo - half : lo - half + 128, :]
            else:
                x = jnp.concatenate([g0_ref[lo:half, :], g1_ref[0 : lo + 128 - half, :]], axis=0)
            gt_ref[:, lo : lo + 128] = x.astype(F32).T.astype(BF16)

    p = jnp.dot(gt_ref[:, :VL], w_ref[...], preferred_element_type=F32).astype(BF16)
    even = pos[3] == 0
    for z in range(4):
        first, second = p[:, 256 * z : 256 * z + 128], p[:, 256 * z + 128 : 256 * z + 256]
        mine_ref[0, z] = jnp.where(even, first, second)
        other_ref[0, z] = jnp.where(even, second, first)


def hidden_chunk(pos, g0, g1, wt):
    out = pl.BlockSpec((1, 4, TC, 128), lambda i, p: (i, 0, 0, 0))
    return call(
        hidden_body,
        out_shape=[jax.ShapeDtypeStruct((4, 4, TC, 128), BF16)] * 2,
        grid_spec=pltpu.PrefetchScalarGridSpec(
            num_scalar_prefetch=1,
            grid=(4,),
            in_specs=[whole((VP // 2, TC))] * 2 + [pl.BlockSpec((VL, 1024), lambda i, p: (0, i))],
            out_specs=[out, out],
            scratch_shapes=[pltpu.VMEM((TC, VP), BF16)],
        ),
        cost=(2 * VP * TC * D, VP * D * 2 + 4 * MIB),
    )(pos, g0, g1, wt)


def head_body(count, pos, *refs):
    g_refs, h_ref, out_ref, k_ref = refs[:4], refs[4], refs[-2], refs[-1]

    @pl.when(pl.program_id(0) == 0)
    def _():
        for s in range(4):
            group = (pos[0] + 4 - s) % 4
            for j in range(8):
                k_ref[s * TC : (s + 1) * TC, j * 128 : (j + 1) * 128] = h_ref[group * 8 + j]

    g = jnp.concatenate([r[...] for r in g_refs], axis=1)
    total = jnp.dot(g, k_ref[...], preferred_element_type=F32)
    if count > 0:
        total = total + refs[5][...].astype(F32)
    out_ref[...] = total.astype(BF16)


def head_chunk(pos, gs, h2, c, prior=None, first=0, steps=NB, other=None):
    specs = [pl.BlockSpec((VB, TC), lambda i, p: (i, 0))] * 4
    specs.append(pl.BlockSpec((NV, TC, 128), lambda i, p: (0, c, 0)))
    args = list(gs) + [h2]
    block = pl.BlockSpec((VB, DX), lambda i, p: (i + first, 0))
    kw = {}
    if prior is not None:
        specs.append(block)
        args.append(prior)
    if other is not None:
        specs.append(pl.BlockSpec(memory_space=pl.ANY))
        args.append(other)
        kw["input_output_aliases"] = {len(args): 0}
    return call(
        functools.partial(head_body, 0 if prior is None else 1),
        out_shape=jax.ShapeDtypeStruct((VP if prior is None else VL, DX), BF16),
        grid_spec=pltpu.PrefetchScalarGridSpec(
            num_scalar_prefetch=1,
            grid=(steps,),
            in_specs=specs,
            out_specs=block,
            scratch_shapes=[pltpu.VMEM((4 * TC, DX), BF16)],
        ),
        cost=(VP * 2048 * DX, 12 * MIB),
        **kw,
    )(pos, *args)


def shift(x, axis, n):
    return lax.ppermute(x, axis, [(i, (i + n) % 4) for i in range(4)])


def swap(x):
    return lax.ppermute(x, "c", [(0, 1), (1, 0)])


def spread(x, axis):
    return [x] + [shift(x, axis, n) for n in (1, 2, 3)]


def gather_hidden(by_z):
    by_y = jnp.stack(spread(by_z, "y"))
    return by_y, swap(by_y)


def chip_sum(mine, other):
    return (mine.astype(F32) + swap(other).astype(F32)).astype(BF16)


def reduce_hidden(both):
    got = lax.all_to_all(both.reshape(16, TC, 128), ("y", "z"), 0, 0, tiled=True)
    return jnp.sum(got.astype(F32), axis=0).astype(BF16)


def after(x, *others):
    return lax.optimization_barrier((x,) + others)[0]


def per_device(hidden, head_weight, teacher_logits, row_weight):
    pos = jnp.stack([lax.axis_index(a) for a in ("x", "y", "z", "c")]).astype(jnp.int32)
    wt = head_weight.T
    rows = hidden.reshape(NV, NCH, 8, 128)
    chunks = [rows[:, c].reshape(TC, 128) for c in range(NCH)]
    weights = row_weight.reshape(NV, NCH, 8)
    weights = [weights[:, c].reshape(1, TC) for c in range(NCH)]

    both = jnp.concatenate(chunks, axis=0)
    blocks = prep(teacher_logits)
    teacher0 = lax.all_to_all(blocks[0], V, 0, 0, tiled=True)
    by_z = after(jnp.stack(spread(both, "z")), blocks[0])
    own0, sib0 = gather_hidden(by_z[:, :TC])
    own1, sib1 = gather_hidden(after(by_z[:, TC:], own0))
    s0, m0 = student_chunk(pos, wt, own0, sib0)
    teacher1 = lax.all_to_all(after(blocks[1], teacher0), V, 0, 0, tiled=True)
    t0, x = stats_chunk(after(s0, own1), m0, teacher0)
    x = merge([x, swap(x)])
    xs = spread(x, "z")
    part = student_chunk(after(pos, x), wt, own1, sib1, 0, NB // 2)
    x = merge([after(xs[0], part[1])] + xs[1:])
    xs = spread(x, "y")
    s1, m1 = student_chunk(after(pos, x), wt, own1, sib1, NB // 2, NB // 2, part)

    across = lax.ppermute(both, ("x", "y"), [(x * 4 + y, y * 4 + x) for x in range(4) for y in range(4)])
    h2 = lax.all_gather(after(across, x), V)

    *g0, kl0 = grad_chunk(xs, after(weights[0], m1), s0, t0)
    upper0 = spread(g0[0], "x")
    lower0 = spread(after(g0[1], *upper0), "x")
    t1, x = stats_chunk(after(s1, kl0), m1, teacher1)
    x = lax.all_to_all(jnp.broadcast_to(x, (NV, 8, TC)), V, 0, 0, tiled=True)
    part0 = hidden_chunk(after(pos, t1, *upper0), *g0, wt)
    sum0 = chip_sum(part0[0], after(part0[1], x))
    share0 = reduce_hidden(sum0)
    *g1, kl1 = grad_chunk([x], after(weights[1], part0[0], *lower0), s1, t1)
    upper1 = spread(g1[0], "x")
    lower1 = spread(after(g1[1], *upper1), "x")
    part1 = hidden_chunk(pos, *g1, wt)
    share1 = reduce_hidden(chip_sum(part1[0], after(part1[1], share0, *upper1)))
    head = head_chunk(after(pos, part1[0], *upper1), upper0, h2, 0, None, 0, NB // 2)
    head = head_chunk(pos, lower0, h2, 0, None, NB // 2, NB // 2, head)
    done = head_chunk(pos, upper1, h2, 1, head, 0, NB // 2)
    head = head_chunk(pos, lower1, h2, 1, head, NB // 2, NB // 2, done)
    shares, kls = [share0, share1], [kl0, kl1]

    kl_rows = jnp.stack([k.reshape(NV, 8) for k in kls], axis=1).reshape(512)
    grad_hidden = jnp.stack([s.reshape(NV, 8, 128) for s in shares], axis=1).reshape(512, 128)
    return kl_rows, grad_hidden, head.T


def solution(mesh):
    fine = Mesh(mesh.devices.reshape(4, 4, 4, 2), ("x",) + V)
    in_specs = (P("x", V), P(None, V), P(("x",) + V, None), P("x"))
    out_specs = (P("x"), P("x", V), P("x", V))
    return jax.shard_map(per_device, mesh=fine, in_specs=in_specs, out_specs=out_specs, check_vma=False)
```

```python
import functools

import jax
import jax.numpy as jnp
from jax import lax
from jax.experimental import pallas as pl
from jax.experimental.pallas import tpu as pltpu
from jax.sharding import Mesh
from jax.sharding import PartitionSpec as P

F32, BF16 = jnp.float32, jnp.bfloat16
V = ("y", "z", "c")
NV = 32
VL = 2374
KT = 19
SB = 512
NS = 5
GB = 608
VP = 2432
CUTS = ((0, 2), (2, 1), (3, 1))
T = 512
D = 4096
DX = 1024
LOW = -1e30
MIB = 1 << 20


def call(body, limit=60, **kw):
    return pl.pallas_call(
        body,
        compiler_params=pltpu.CompilerParams(vmem_limit_bytes=limit * MIB),
        cost_estimate=pl.CostEstimate(flops=1 << 20, bytes_accessed=1 << 16, transcendentals=0),
        **kw,
    )


def whole(shape):
    return pl.BlockSpec(shape, lambda *_: (0,) * len(shape))


def prep_body(t_ref, out_ref):
    end = NV * VL
    for i in range(NV):
        for k in range(KT):
            start = VL * i + 128 * k
            if start + 128 <= end:
                out_ref[i, k] = t_ref[:, start : start + 128]
            else:
                tile = t_ref[:, end - 128 : end].astype(F32)
                out_ref[i, k] = pltpu.roll(tile, end - start, axis=1).astype(BF16)


def prep(teacher):
    shape = (NV, KT, 16, 128)
    return call(
        prep_body,
        out_shape=jax.ShapeDtypeStruct(shape, BF16),
        grid=(1,),
        in_specs=[whole(teacher.shape)],
        out_specs=whole(shape),
    )(teacher)


def fold(x, op):
    return op(x.reshape(-1, 8, T), axis=0)


def student_body(pos, w_ref, own_ref, sib_ref, s_ref, m_ref, l_ref, h_ref):
    step = pl.program_id(0)

    @pl.when(step == 0)
    def _():
        for a in range(4):
            for b in range(4):
                for ref, c in ((own_ref, pos[3]), (sib_ref, 1 - pos[3])):
                    y = (pos[1] + 4 - jnp.where(c == 0, a, b)) % 4
                    z = (pos[2] + 4 - jnp.where(c == 0, b, a)) % 4
                    at = pl.multiple_of(((y * 4 + z) * 2 + c) * 128, 128)
                    h_ref[:, pl.ds(at, 128)] = ref[a, b]
        m_ref[...] = jnp.full_like(m_ref, LOW)
        l_ref[...] = jnp.zeros_like(l_ref)

    s = lax.dot_general(w_ref[...], h_ref[...], (((1,), (1,)), ((), ())), preferred_element_type=F32)
    rows = step * SB + lax.broadcasted_iota(jnp.int32, s.shape, 0)
    s = jnp.where(rows < VL, s, LOW)
    s_ref[...] = s
    old = m_ref[...]
    peak = jnp.maximum(old, fold(s, jnp.max))
    m_ref[...] = peak
    es = jnp.exp(s.reshape(-1, 8, T) - peak[None])
    l_ref[...] = l_ref[...] * jnp.exp(old - peak) + jnp.sum(es, axis=0)


def student(pos, wt, own, sib):
    part = jax.ShapeDtypeStruct((8, T), F32)
    return call(
        student_body,
        out_shape=[jax.ShapeDtypeStruct((NS * SB, T), F32), part, part],
        grid_spec=pltpu.PrefetchScalarGridSpec(
            num_scalar_prefetch=1,
            grid=(NS,),
            in_specs=[
                pl.BlockSpec((SB, D), lambda i, p: (i, 0)),
                whole((4, 4, T, 128)),
                whole((4, 4, T, 128)),
            ],
            out_specs=[pl.BlockSpec((SB, T), lambda i, p: (i, 0)), whole((8, T)), whole((8, T))],
            scratch_shapes=[pltpu.VMEM((T, D), BF16)],
        ),
    )(pos, wt, own, sib)


def stats_body(m_ref, l_ref, s_ref, t_ref, tt_ref, out_ref, p_ref, sum_ref, cross_ref):
    step = pl.program_id(0)

    @pl.when(step == 0)
    def _():
        p_ref[...] = jnp.full_like(p_ref, LOW)
        sum_ref[...] = jnp.zeros_like(sum_ref)
        cross_ref[...] = jnp.zeros_like(cross_ref)

    for n in range(SB // 128):

        @pl.when(step * (SB // 128) + n < KT)
        def _():
            t = t_ref[:, n].reshape(T, 128).astype(F32).T
            rows = step * SB + n * 128 + lax.broadcasted_iota(jnp.int32, t.shape, 0)
            t = jnp.where(rows < VL, t, LOW)
            tt_ref[n * 128 : (n + 1) * 128, :] = t.astype(BF16)
            old = p_ref[...]
            peak = jnp.maximum(old, fold(t, jnp.max))
            p_ref[...] = peak
            scale = jnp.exp(old - peak)
            t = t.reshape(-1, 8, T)
            et = jnp.exp(t - peak[None])
            s = s_ref[n * 128 : (n + 1) * 128, :].reshape(-1, 8, T)
            sum_ref[...] = sum_ref[...] * scale + jnp.sum(et, axis=0)
            cross_ref[...] = cross_ref[...] * scale + jnp.sum(et * (t - s), axis=0)

    @pl.when(step == NS - 1)
    def _():
        s_peak = jnp.max(m_ref[...], axis=0, keepdims=True)
        t_peak = jnp.max(p_ref[...], axis=0, keepdims=True)
        se, te = jnp.exp(m_ref[...] - s_peak), jnp.exp(p_ref[...] - t_peak)
        total = lambda scale, ref: jnp.sum(scale * ref[...], axis=0, keepdims=True)
        values = [s_peak, t_peak, total(se, l_ref), total(te, sum_ref), total(te, cross_ref)]
        row = lax.broadcasted_iota(jnp.int32, (8, T), 0)
        out = jnp.zeros((8, T), F32)
        for n, v in enumerate(values):
            out = jnp.where(row == n, v, out)
        for i in range(NV):
            out_ref[i] = out


def stats(m, l, s, t):
    block = pl.BlockSpec((SB, T), lambda i: (i, 0))
    return call(
        stats_body,
        out_shape=[jax.ShapeDtypeStruct((NS * SB, T), BF16), jax.ShapeDtypeStruct((NV, 8, T), F32)],
        grid=(NS,),
        in_specs=[
            whole((8, T)),
            whole((8, T)),
            block,
            pl.BlockSpec((NV, SB // 128, 16, 128), lambda i: (0, i, 0, 0)),
        ],
        out_specs=[block, whole((NV, 8, T))],
        scratch_shapes=[pltpu.VMEM((8, T), F32)] * 3,
    )(m, l, s, t)


def grad_body(all_ref, w_ref, s_ref, t_ref, *refs):
    kl_ref, c_ref = refs[-2:]
    step = pl.program_id(0)

    @pl.when(step == 0)
    def _():
        v = all_ref[...]
        s_peak, t_peak = jnp.max(v[:, 0:1, :], axis=0), jnp.max(v[:, 1:2, :], axis=0)
        se, te = jnp.exp(v[:, 0:1, :] - s_peak[None]), jnp.exp(v[:, 1:2, :] - t_peak[None])
        total = lambda scale, n: jnp.sum(scale * v[:, n : n + 1, :], axis=0)
        s_tot, t_tot, cross = total(se, 2), total(te, 3), total(te, 4)
        kl_ref[...] = cross / t_tot - t_peak - jnp.log(t_tot) + s_peak + jnp.log(s_tot)
        c_ref[0:1, :] = s_peak
        c_ref[1:2, :] = t_peak
        c_ref[2:3, :] = w_ref[...] / s_tot
        c_ref[3:4, :] = w_ref[...] / t_tot

    es = jnp.exp(s_ref[...] - c_ref[0:1, :]) * c_ref[2:3, :]
    et = jnp.exp(t_ref[...].astype(F32) - c_ref[1:2, :]) * c_ref[3:4, :]
    g = (es - et).astype(BF16)

    for (first, steps), g_ref in zip(CUTS, refs):

        @pl.when((step >= first) & (step < first + steps))
        def _():
            g_ref[...] = g


def piece(first, steps):
    return pl.BlockSpec((GB, T), lambda i: (jnp.clip(i - first, 0, steps - 1), 0))


def grad(gathered, w, s, t):
    block = pl.BlockSpec((GB, T), lambda i: (i, 0))
    return call(
        grad_body,
        out_shape=[jax.ShapeDtypeStruct((n * GB, T), BF16) for _, n in CUTS] + [jax.ShapeDtypeStruct((1, T), F32)],
        grid=(VP // GB,),
        in_specs=[whole((NV, 8, T)), whole((1, T)), block, block],
        out_specs=[piece(*cut) for cut in CUTS] + [whole((1, T))],
        scratch_shapes=[pltpu.VMEM((8, T), F32)],
    )(gathered, w, s, t)


def hidden_body(pos, *refs):
    g_refs, (w_ref, mine_ref, other_ref, gt_ref) = refs[: len(CUTS)], refs[len(CUTS) :]

    @pl.when(pl.program_id(0) == 0)
    def _():
        for lo in range(0, VP, 128):
            rows = []
            for (first, steps), ref in zip(CUTS, g_refs):
                start, end = max(lo - first * GB, 0), min(lo + 128 - first * GB, steps * GB)
                if start < end:
                    rows.append(ref[start:end, :])
            x = jnp.concatenate(rows, axis=0)
            gt_ref[:, lo : lo + 128] = x.astype(F32).T.astype(BF16)

    p = jnp.dot(gt_ref[:, :VL], w_ref[...], preferred_element_type=F32).astype(BF16)
    even = pos[3] == 0
    for z in range(4):
        first, second = p[:, 256 * z : 256 * z + 128], p[:, 256 * z + 128 : 256 * z + 256]
        mine_ref[0, z] = jnp.where(even, first, second)
        other_ref[0, z] = jnp.where(even, second, first)


def hidden_part(pos, gs, wt):
    out = pl.BlockSpec((1, 4, T, 128), lambda i, p: (i, 0, 0, 0))
    return call(
        hidden_body,
        out_shape=[jax.ShapeDtypeStruct((4, 4, T, 128), BF16)] * 2,
        grid_spec=pltpu.PrefetchScalarGridSpec(
            num_scalar_prefetch=1,
            grid=(4,),
            in_specs=[whole(g.shape) for g in gs] + [pl.BlockSpec((VL, 1024), lambda i, p: (0, i))],
            out_specs=[out, out],
            scratch_shapes=[pltpu.VMEM((T, VP), BF16)],
        ),
    )(pos, *gs, wt)


def head_body(pos, *refs):
    g_refs, (far0, far1, h_ref), out_ref, k_ref = refs[:3], refs[3:6], refs[-2], refs[-1]

    @pl.when(pl.program_id(0) == 0)
    def _():
        for n, away in enumerate((0, 3, 1, 2)):
            group = (pos[0] + away) % 4
            for j in range(8):
                k_ref[n * T : (n + 1) * T, j * 128 : (j + 1) * 128] = h_ref[group * 8 + j]

    if far0.shape[0] < GB:
        far = jnp.concatenate([far0[...], far1[...]], axis=0)
    else:
        far = jnp.where(pl.program_id(0) == 0, far0[...], far1[...])
    g = jnp.concatenate([r[...] for r in g_refs] + [far], axis=1)
    out_ref[...] = jnp.dot(g, k_ref[...], preferred_element_type=F32).astype(BF16)


def head_piece(pos, gs, h2, first, steps, other):
    specs = [pl.BlockSpec((GB, T), lambda i, p: (i, 0))] * 3 + [whole(g.shape) for g in gs[3:]]
    specs.append(whole((NV, T, 128)))
    args = list(gs) + [h2]
    kw = {}
    if other is not None:
        specs.append(pl.BlockSpec(memory_space=pl.ANY))
        args.append(other)
        kw["input_output_aliases"] = {len(args): 0}
    return call(
        head_body,
        out_shape=jax.ShapeDtypeStruct((VL, DX), BF16),
        grid_spec=pltpu.PrefetchScalarGridSpec(
            num_scalar_prefetch=1,
            grid=(steps,),
            in_specs=specs,
            out_specs=pl.BlockSpec((GB, DX), lambda i, p: (i + first, 0)),
            scratch_shapes=[pltpu.VMEM((4 * T, DX), BF16)],
        ),
        **kw,
    )(pos, *args)


def shift(x, n):
    return lax.ppermute(x, "x", [(i, (i + n) % 4) for i in range(4)])


def swap(x):
    return lax.ppermute(x, "c", [(0, 1), (1, 0)])


def spread(x, first):
    got = [x]
    for n in (1, 2, 3):
        pairs = []
        for y in range(4):
            for z in range(4):
                for c in range(2):
                    to = (y, (z + n) % 4) if c == first else ((y + n) % 4, z)
                    pairs.append(((y * 4 + z) * 2 + c, (to[0] * 4 + to[1]) * 2 + c))
        got.append(lax.ppermute(x, V, pairs))
    return jnp.stack(got)


def after(x, *others):
    return lax.optimization_barrier((x,) + others)[0]


def per_device(hidden, head_weight, teacher_logits, row_weight):
    pos = jnp.stack([lax.axis_index(a) for a in ("x", "y", "z", "c")]).astype(jnp.int32)
    wt = head_weight.T
    blocks = prep(teacher_logits)
    teacher = lax.all_to_all(blocks, V, 0, 0, tiled=True)
    one = spread(hidden, 0)
    own = spread(after(one, blocks), 1)
    sib = swap(own)
    s, m, l = student(pos, wt, own, sib)
    t, share = stats(m, l, s, teacher)
    gathered = lax.all_to_all(share, V, 0, 0, tiled=True)

    across = lax.ppermute(hidden, ("x", "y"), [(x * 4 + y, y * 4 + x) for x in range(4) for y in range(4)])
    h2 = lax.all_gather(after(across, share), V)

    *gs, kl = grad(gathered, row_weight.reshape(1, T), s, t)
    pieces = []
    for g in gs:
        if pieces:
            g = after(g, pieces[-1][1], pieces[-1][2])
        left, right = shift(g, 1), shift(g, 3)
        half = g.shape[0] // 2
        pieces.append([g, left, right, shift(left[:half], 1), shift(right[half:], 3)])
    mine, other = hidden_part(pos, gs, wt)
    both = (mine.astype(F32) + swap(after(other, *pieces[0][1:3])).astype(F32)).astype(BF16)
    both = after(both, *pieces[1][1:3])
    got = lax.all_to_all(both.reshape(16, T, 128), ("y", "z"), 0, 0, tiled=True)
    grad_hidden = jnp.sum(got.astype(F32), axis=0).astype(BF16)

    head = None
    for cut, parts in zip(CUTS, pieces):
        head = head_piece(pos, parts, h2, *cut, head)
    return kl.reshape(T), grad_hidden, head.T


def solution(mesh):
    fine = Mesh(mesh.devices.reshape(4, 4, 4, 2), ("x",) + V)
    in_specs = (P("x", V), P(None, V), P(("x",) + V, None), P("x"))
    out_specs = (P("x"), P("x", V), P("x", V))
    return jax.shard_map(per_device, mesh=fine, in_specs=in_specs, out_specs=out_specs, check_vma=False)
```

```python
import functools

import jax
import jax.numpy as jnp
from jax import lax
from jax.experimental import pallas as pl
from jax.experimental.pallas import tpu as pltpu
from jax.sharding import Mesh
from jax.sharding import PartitionSpec as P

F32, BF16 = jnp.float32, jnp.bfloat16
V = ("y", "z", "c")
NV = 32
VL = 2374
KT = 19
SB = 512
NS = 5
GB = 608
VP = 2432
CUTS = ((0, 2), (2, 1), (3, 1))
T = 512
D = 4096
DX = 1024
LOW = -1e30
MIB = 1 << 20


def call(body, **kw):
    return pl.pallas_call(
        body,
        compiler_params=pltpu.CompilerParams(vmem_limit_bytes=60 * MIB),
        cost_estimate=pl.CostEstimate(flops=1 << 20, bytes_accessed=1 << 16, transcendentals=0),
        **kw,
    )


def whole(shape):
    return pl.BlockSpec(shape, lambda *_: (0,) * len(shape))


def prep_body(t_ref, out_ref):
    end = NV * VL
    for i in range(NV):
        for k in range(KT):
            start = VL * i + 128 * k
            if start + 128 <= end:
                out_ref[i, k] = t_ref[:, start : start + 128]
            else:
                tile = t_ref[:, end - 128 : end].astype(F32)
                out_ref[i, k] = pltpu.roll(tile, end - start, axis=1).astype(BF16)


def prep(teacher):
    shape = (NV, KT, 16, 128)
    return call(
        prep_body,
        out_shape=jax.ShapeDtypeStruct(shape, BF16),
        grid=(1,),
        in_specs=[whole(teacher.shape)],
        out_specs=whole(shape),
    )(teacher)


def fold(x, op):
    return op(x.reshape(-1, 8, T), axis=0)


def student_body(pos, w_ref, *refs):
    own_refs, sib_refs, (s_ref, m_ref, l_ref, h_ref) = refs[:4], refs[4:8], refs[8:]
    step = pl.program_id(0)

    @pl.when(step == 0)
    def _():
        for a in range(4):
            for b in range(4):
                for ref, c in ((own_refs[a], pos[3]), (sib_refs[a], 1 - pos[3])):
                    y = (pos[1] + 4 - jnp.where(c == 0, a, b)) % 4
                    z = (pos[2] + 4 - jnp.where(c == 0, b, a)) % 4
                    at = pl.multiple_of(((y * 4 + z) * 2 + c) * 128, 128)
                    h_ref[:, pl.ds(at, 128)] = ref[b]
        m_ref[...] = jnp.full_like(m_ref, LOW)
        l_ref[...] = jnp.zeros_like(l_ref)

    s = lax.dot_general(w_ref[...], h_ref[...], (((1,), (1,)), ((), ())), preferred_element_type=F32)
    rows = step * SB + lax.broadcasted_iota(jnp.int32, s.shape, 0)
    s = jnp.where(rows < VL, s, LOW)
    s_ref[...] = s
    old = m_ref[...]
    peak = jnp.maximum(old, fold(s, jnp.max))
    m_ref[...] = peak
    es = jnp.exp(s.reshape(-1, 8, T) - peak[None])
    l_ref[...] = l_ref[...] * jnp.exp(old - peak) + jnp.sum(es, axis=0)


def student(pos, wt, own, sib):
    part = jax.ShapeDtypeStruct((8, T), F32)
    return call(
        student_body,
        out_shape=[jax.ShapeDtypeStruct((NS * SB, T), F32), part, part],
        grid_spec=pltpu.PrefetchScalarGridSpec(
            num_scalar_prefetch=1,
            grid=(NS,),
            in_specs=[pl.BlockSpec((SB, D), lambda i, p: (i, 0))] + [whole((4, T, 128))] * 8,
            out_specs=[pl.BlockSpec((SB, T), lambda i, p: (i, 0)), whole((8, T)), whole((8, T))],
            scratch_shapes=[pltpu.VMEM((T, D), BF16)],
        ),
    )(pos, wt, *own, *sib)


def stats_body(m_ref, l_ref, s_ref, t_ref, tt_ref, out_ref, p_ref, sum_ref, cross_ref):
    step = pl.program_id(0)

    @pl.when(step == 0)
    def _():
        p_ref[...] = jnp.full_like(p_ref, LOW)
        sum_ref[...] = jnp.zeros_like(sum_ref)
        cross_ref[...] = jnp.zeros_like(cross_ref)

    for n in range(SB // 128):

        @pl.when(step * (SB // 128) + n < KT)
        def _():
            t = t_ref[:, n].reshape(T, 128).astype(F32).T
            rows = step * SB + n * 128 + lax.broadcasted_iota(jnp.int32, t.shape, 0)
            t = jnp.where(rows < VL, t, LOW)
            tt_ref[n * 128 : (n + 1) * 128, :] = t.astype(BF16)
            old = p_ref[...]
            peak = jnp.maximum(old, fold(t, jnp.max))
            p_ref[...] = peak
            scale = jnp.exp(old - peak)
            t = t.reshape(-1, 8, T)
            et = jnp.exp(t - peak[None])
            s = s_ref[n * 128 : (n + 1) * 128, :].reshape(-1, 8, T)
            sum_ref[...] = sum_ref[...] * scale + jnp.sum(et, axis=0)
            cross_ref[...] = cross_ref[...] * scale + jnp.sum(et * (t - s), axis=0)

    @pl.when(step == NS - 1)
    def _():
        s_peak = jnp.max(m_ref[...], axis=0, keepdims=True)
        t_peak = jnp.max(p_ref[...], axis=0, keepdims=True)
        se, te = jnp.exp(m_ref[...] - s_peak), jnp.exp(p_ref[...] - t_peak)
        total = lambda scale, ref: jnp.sum(scale * ref[...], axis=0, keepdims=True)
        values = [s_peak, t_peak, total(se, l_ref), total(te, sum_ref), total(te, cross_ref)]
        row = lax.broadcasted_iota(jnp.int32, (8, T), 0)
        out = jnp.zeros((8, T), F32)
        for n, v in enumerate(values):
            out = jnp.where(row == n, v, out)
        for i in range(NV):
            out_ref[i] = out


def stats(m, l, s, t):
    block = pl.BlockSpec((SB, T), lambda i: (i, 0))
    return call(
        stats_body,
        out_shape=[jax.ShapeDtypeStruct((NS * SB, T), BF16), jax.ShapeDtypeStruct((NV, 8, T), F32)],
        grid=(NS,),
        in_specs=[
            whole((8, T)),
            whole((8, T)),
            block,
            pl.BlockSpec((NV, SB // 128, 16, 128), lambda i: (0, i, 0, 0)),
        ],
        out_specs=[block, whole((NV, 8, T))],
        scratch_shapes=[pltpu.VMEM((8, T), F32)] * 3,
    )(m, l, s, t)


def grad_body(cuts, all_ref, w_ref, s_ref, t_ref, *refs):
    kl_ref, c_ref = refs[-2:]
    step = pl.program_id(0)

    @pl.when(step == 0)
    def _():
        v = all_ref[...]
        s_peak, t_peak = jnp.max(v[:, 0:1, :], axis=0), jnp.max(v[:, 1:2, :], axis=0)
        se, te = jnp.exp(v[:, 0:1, :] - s_peak[None]), jnp.exp(v[:, 1:2, :] - t_peak[None])
        total = lambda scale, n: jnp.sum(scale * v[:, n : n + 1, :], axis=0)
        s_tot, t_tot, cross = total(se, 2), total(te, 3), total(te, 4)
        kl_ref[...] = cross / t_tot - t_peak - jnp.log(t_tot) + s_peak + jnp.log(s_tot)
        c_ref[0:1, :] = s_peak
        c_ref[1:2, :] = t_peak
        c_ref[2:3, :] = w_ref[...] / s_tot
        c_ref[3:4, :] = w_ref[...] / t_tot

    es = jnp.exp(s_ref[...] - c_ref[0:1, :]) * c_ref[2:3, :]
    et = jnp.exp(t_ref[...].astype(F32) - c_ref[1:2, :]) * c_ref[3:4, :]
    g = (es - et).astype(BF16)
    at = step + cuts[0][0]
    for (first, steps), g_ref in zip(cuts, refs):

        @pl.when((at >= first) & (at < first + steps))
        def _():
            g_ref[...] = g


def piece(start, first, steps):
    return pl.BlockSpec((GB, T), lambda i: (jnp.clip(i + start - first, 0, steps - 1), 0))


def grad(gathered, w, s, t, cuts):
    start = cuts[0][0]
    block = pl.BlockSpec((GB, T), lambda i: (i + start, 0))
    return call(
        functools.partial(grad_body, cuts),
        out_shape=[jax.ShapeDtypeStruct((n * GB, T), BF16) for _, n in cuts] + [jax.ShapeDtypeStruct((1, T), F32)],
        grid=(sum(n for _, n in cuts),),
        in_specs=[whole((NV, 8, T)), whole((1, T)), block, block],
        out_specs=[piece(start, *cut) for cut in cuts] + [whole((1, T))],
        scratch_shapes=[pltpu.VMEM((8, T), F32)],
    )(gathered, w, s, t)


def hidden_body(pos, *refs):
    g_refs, (w_ref, mine_ref, other_ref, gt_ref) = refs[: len(CUTS)], refs[len(CUTS) :]

    @pl.when(pl.program_id(0) == 0)
    def _():
        for lo in range(0, VP, 128):
            rows = []
            for (first, steps), ref in zip(CUTS, g_refs):
                start, end = max(lo - first * GB, 0), min(lo + 128 - first * GB, steps * GB)
                if start < end:
                    rows.append(ref[start:end, :])
            x = jnp.concatenate(rows, axis=0)
            gt_ref[:, lo : lo + 128] = x.astype(F32).T.astype(BF16)

    p = jnp.dot(gt_ref[:, :VL], w_ref[...], preferred_element_type=F32).astype(BF16)
    even = pos[3] == 0
    for z in range(4):
        first, second = p[:, 256 * z : 256 * z + 128], p[:, 256 * z + 128 : 256 * z + 256]
        mine_ref[0, z] = jnp.where(even, first, second)
        other_ref[0, z] = jnp.where(even, second, first)


def hidden_part(pos, gs, wt):
    out = pl.BlockSpec((1, 4, T, 128), lambda i, p: (i, 0, 0, 0))
    return call(
        hidden_body,
        out_shape=[jax.ShapeDtypeStruct((4, 4, T, 128), BF16)] * 2,
        grid_spec=pltpu.PrefetchScalarGridSpec(
            num_scalar_prefetch=1,
            grid=(4,),
            in_specs=[whole(g.shape) for g in gs] + [pl.BlockSpec((VL, 1024), lambda i, p: (0, i))],
            out_specs=[out, out],
            scratch_shapes=[pltpu.VMEM((T, VP), BF16)],
        ),
    )(pos, *gs, wt)


def tokens_body(pos, h_ref, k_ref):
    for j in range(8):
        k_ref[:, j * 128 : (j + 1) * 128] = h_ref[j]


def tokens(pos, h2):
    group = lambda i, p: (p[0] + jnp.where(i == 0, 0, jnp.where(i == 1, 3, i - 1))) % 4
    return call(
        tokens_body,
        out_shape=jax.ShapeDtypeStruct((4 * T, DX), BF16),
        grid_spec=pltpu.PrefetchScalarGridSpec(
            num_scalar_prefetch=1,
            grid=(4,),
            in_specs=[pl.BlockSpec((8, T, 128), lambda i, p: (group(i, p), 0, 0))],
            out_specs=pl.BlockSpec((T, DX), lambda i, p: (i, 0)),
        ),
    )(pos, h2)


def head_body(near, far, prior, *refs):
    refs = list(refs)
    parts = [refs.pop(0)[...] for _ in range(3)] if near else []
    if far:
        far0, far1 = refs.pop(0), refs.pop(0)
        if far0.shape[0] < GB:
            parts.append(jnp.concatenate([far0[...], far1[...]], axis=0))
        else:
            parts.append(jnp.where(pl.program_id(0) == 0, far0[...], far1[...]))
    total = jnp.dot(jnp.concatenate(parts, axis=1), refs.pop(0)[...], preferred_element_type=F32)
    if prior:
        total = total + refs.pop(0)[...]
    refs[-1][...] = total.astype(refs[-1].dtype)


def head_piece(near, far, k, first, steps, prior=None, other=None):
    specs = [pl.BlockSpec((GB, T), lambda i: (i, 0))] * len(near) + [whole(g.shape) for g in far]
    rows = T * (len(near) + len(far) // 2)
    specs.append(pl.BlockSpec((rows, DX), lambda i: (0 if near else 3, 0)))
    args = [*near, *far, k]
    kw = {}
    if prior is not None:
        specs.append(pl.BlockSpec((GB, DX), lambda i: (i, 0)))
        args.append(prior)
    if other is not None:
        specs.append(pl.BlockSpec(memory_space=pl.ANY))
        args.append(other)
        kw["input_output_aliases"] = {len(args) - 1: 0}
    if far:
        out = jax.ShapeDtypeStruct((VL, DX), BF16)
    else:
        out, first = jax.ShapeDtypeStruct((steps * GB, DX), F32), 0
    return call(
        functools.partial(head_body, bool(near), bool(far), prior is not None),
        out_shape=out,
        grid=(steps,),
        in_specs=specs,
        out_specs=pl.BlockSpec((GB, DX), lambda i: (i + first, 0)),
        **kw,
    )(*args)


def shift(x, n):
    return lax.ppermute(x, "x", [(i, (i + n) % 4) for i in range(4)])


def swap(x):
    return lax.ppermute(x, "c", [(0, 1), (1, 0)])


def spread(x, first):
    got = [x]
    for n in (1, 2, 3):
        pairs = []
        for y in range(4):
            for z in range(4):
                for c in range(2):
                    to = (y, (z + n) % 4) if c == first else ((y + n) % 4, z)
                    pairs.append(((y * 4 + z) * 2 + c, (to[0] * 4 + to[1]) * 2 + c))
        got.append(lax.ppermute(x, V, pairs))
    return got


def after(x, *others):
    return lax.optimization_barrier((x,) + others)[0]


def per_device(hidden, head_weight, teacher_logits, row_weight):
    pos = jnp.stack([lax.axis_index(a) for a in ("x", "y", "z", "c")]).astype(jnp.int32)
    wt = head_weight.T
    blocks = prep(teacher_logits)
    one = jnp.stack(spread(hidden, 0))
    own = spread(after(one, blocks), 1)
    teacher = lax.all_to_all(blocks, V, 0, 0, tiled=True)
    s, m, l = student(pos, wt, own, [swap(x) for x in own])
    t, share = stats(m, l, s, teacher)
    gathered = lax.all_to_all(share, V, 0, 0, tiled=True)

    w = row_weight.reshape(1, T)
    gu, kl = grad(gathered, w, s, t, CUTS[:1])
    gm, gl, _ = grad(gathered, after(w, gu), s, t, CUTS[1:])
    across = lax.ppermute(hidden, ("x", "y"), [(x * 4 + y, y * 4 + x) for x in range(4) for y in range(4)])
    h2 = lax.all_gather(after(across, kl), V)

    def ring(g):
        left, right = shift(g, 1), shift(g, 3)
        half = g.shape[0] // 2
        return [g, left, right], [shift(left[:half], 1), shift(right[half:], 3)]

    near_u, far_u = ring(gu)
    near_m, far_m = ring(gm)
    near_l, far_l = ring(after(gl, *near_m))
    mine, other = hidden_part(pos, (gu, gm, gl), wt)
    both = (mine.astype(F32) + swap(after(other, *near_u)).astype(F32)).astype(BF16)
    both = after(both, *near_m)
    got = lax.all_to_all(both.reshape(16, T, 128), ("y", "z"), 0, 0, tiled=True)
    grad_hidden = jnp.sum(got.astype(F32), axis=0).astype(BF16)

    k = tokens(pos, h2)
    head = head_piece(near_u, far_u, k, *CUTS[0])
    head = head_piece(near_m, far_m, k, *CUTS[1], other=head)
    part = head_piece(near_l, [], k, *CUTS[2])
    head = head_piece([], far_l, k, *CUTS[2], prior=part, other=head)
    return kl.reshape(T), grad_hidden, head.T


def solution(mesh):
    fine = Mesh(mesh.devices.reshape(4, 4, 4, 2), ("x",) + V)
    in_specs = (P("x", V), P(None, V), P(("x",) + V, None), P("x"))
    out_specs = (P("x"), P("x", V), P("x", V))
    return jax.shard_map(per_device, mesh=fine, in_specs=in_specs, out_specs=out_specs, check_vma=False)
```

```python
import functools

import jax
import jax.numpy as jnp
from jax import lax
from jax.experimental import pallas as pl
from jax.experimental.pallas import tpu as pltpu
from jax.sharding import Mesh
from jax.sharding import PartitionSpec as P

F32, BF16 = jnp.float32, jnp.bfloat16
V = ("y", "z", "c")
NV = 32
VL = 2374
KT = 19
SB = 512
NS = 5
GB = 608
VP = 2432
CUTS = ((0, 2), (2, 1), (3, 1))
T = 512
D = 4096
DX = 1024
LOW = -1e30
MIB = 1 << 20


def call(body, **kw):
    return pl.pallas_call(
        body,
        compiler_params=pltpu.CompilerParams(vmem_limit_bytes=60 * MIB),
        cost_estimate=pl.CostEstimate(flops=1 << 20, bytes_accessed=1 << 16, transcendentals=0),
        **kw,
    )


def whole(shape):
    return pl.BlockSpec(shape, lambda *_: (0,) * len(shape))


def prep_body(t_ref, out_ref):
    end = NV * VL
    for i in range(NV):
        for k in range(KT):
            start = VL * i + 128 * k
            if start + 128 <= end:
                out_ref[i, k] = t_ref[:, start : start + 128]
            else:
                tile = t_ref[:, end - 128 : end].astype(F32)
                out_ref[i, k] = pltpu.roll(tile, end - start, axis=1).astype(BF16)


def prep(teacher):
    shape = (NV, KT, 16, 128)
    return call(
        prep_body,
        out_shape=jax.ShapeDtypeStruct(shape, BF16),
        grid=(1,),
        in_specs=[whole(teacher.shape)],
        out_specs=whole(shape),
    )(teacher)


def fold(x, op):
    return op(x.reshape(-1, 8, T), axis=0)


def student_body(pos, w_ref, *refs):
    own_refs, sib_refs, (s_ref, m_ref, l_ref, h_ref) = refs[:4], refs[4:8], refs[8:]
    step = pl.program_id(0)

    @pl.when(step == 0)
    def _():
        for a in range(4):
            for b in range(4):
                for ref, c in ((own_refs[a], pos[3]), (sib_refs[a], 1 - pos[3])):
                    y = (pos[1] + 4 - jnp.where(c == 0, a, b)) % 4
                    z = (pos[2] + 4 - jnp.where(c == 0, b, a)) % 4
                    at = pl.multiple_of(((y * 4 + z) * 2 + c) * 128, 128)
                    h_ref[:, pl.ds(at, 128)] = ref[b]
        m_ref[...] = jnp.full_like(m_ref, LOW)
        l_ref[...] = jnp.zeros_like(l_ref)

    s = lax.dot_general(w_ref[...], h_ref[...], (((1,), (1,)), ((), ())), preferred_element_type=F32)
    rows = step * SB + lax.broadcasted_iota(jnp.int32, s.shape, 0)
    s = jnp.where(rows < VL, s, LOW)
    s_ref[...] = s
    old = m_ref[...]
    peak = jnp.maximum(old, fold(s, jnp.max))
    m_ref[...] = peak
    es = jnp.exp(s.reshape(-1, 8, T) - peak[None])
    l_ref[...] = l_ref[...] * jnp.exp(old - peak) + jnp.sum(es, axis=0)


def student(pos, wt, own, sib):
    part = jax.ShapeDtypeStruct((8, T), F32)
    return call(
        student_body,
        out_shape=[jax.ShapeDtypeStruct((NS * SB, T), F32), part, part],
        grid_spec=pltpu.PrefetchScalarGridSpec(
            num_scalar_prefetch=1,
            grid=(NS,),
            in_specs=[pl.BlockSpec((SB, D), lambda i, p: (i, 0))] + [whole((4, T, 128))] * 8,
            out_specs=[pl.BlockSpec((SB, T), lambda i, p: (i, 0)), whole((8, T)), whole((8, T))],
            scratch_shapes=[pltpu.VMEM((T, D), BF16)],
        ),
    )(pos, wt, *own, *sib)


def stats_body(m_ref, l_ref, s_ref, t_ref, tt_ref, out_ref, p_ref, sum_ref, cross_ref):
    step = pl.program_id(0)

    @pl.when(step == 0)
    def _():
        p_ref[...] = jnp.full_like(p_ref, LOW)
        sum_ref[...] = jnp.zeros_like(sum_ref)
        cross_ref[...] = jnp.zeros_like(cross_ref)

    for n in range(SB // 128):

        @pl.when(step * (SB // 128) + n < KT)
        def _():
            t = t_ref[:, n].reshape(T, 128).astype(F32).T
            rows = step * SB + n * 128 + lax.broadcasted_iota(jnp.int32, t.shape, 0)
            t = jnp.where(rows < VL, t, LOW)
            tt_ref[n * 128 : (n + 1) * 128, :] = t.astype(BF16)
            old = p_ref[...]
            peak = jnp.maximum(old, fold(t, jnp.max))
            p_ref[...] = peak
            scale = jnp.exp(old - peak)
            t = t.reshape(-1, 8, T)
            et = jnp.exp(t - peak[None])
            s = s_ref[n * 128 : (n + 1) * 128, :].reshape(-1, 8, T)
            sum_ref[...] = sum_ref[...] * scale + jnp.sum(et, axis=0)
            cross_ref[...] = cross_ref[...] * scale + jnp.sum(et * (t - s), axis=0)

    @pl.when(step == NS - 1)
    def _():
        s_peak = jnp.max(m_ref[...], axis=0, keepdims=True)
        t_peak = jnp.max(p_ref[...], axis=0, keepdims=True)
        se, te = jnp.exp(m_ref[...] - s_peak), jnp.exp(p_ref[...] - t_peak)
        total = lambda scale, ref: jnp.sum(scale * ref[...], axis=0, keepdims=True)
        values = [s_peak, t_peak, total(se, l_ref), total(te, sum_ref), total(te, cross_ref)]
        row = lax.broadcasted_iota(jnp.int32, (8, T), 0)
        out = jnp.zeros((8, T), F32)
        for n, v in enumerate(values):
            out = jnp.where(row == n, v, out)
        for i in range(NV):
            out_ref[i] = out


def stats(m, l, s, t):
    block = pl.BlockSpec((SB, T), lambda i: (i, 0))
    return call(
        stats_body,
        out_shape=[jax.ShapeDtypeStruct((NS * SB, T), BF16), jax.ShapeDtypeStruct((NV, 8, T), F32)],
        grid=(NS,),
        in_specs=[
            whole((8, T)),
            whole((8, T)),
            block,
            pl.BlockSpec((NV, SB // 128, 16, 128), lambda i: (0, i, 0, 0)),
        ],
        out_specs=[block, whole((NV, 8, T))],
        scratch_shapes=[pltpu.VMEM((8, T), F32)] * 3,
    )(m, l, s, t)


def grad_body(cuts, all_ref, w_ref, s_ref, t_ref, *refs):
    kl_ref, c_ref = refs[-2:]
    step = pl.program_id(0)

    @pl.when(step == 0)
    def _():
        v = all_ref[...]
        s_peak, t_peak = jnp.max(v[:, 0:1, :], axis=0), jnp.max(v[:, 1:2, :], axis=0)
        se, te = jnp.exp(v[:, 0:1, :] - s_peak[None]), jnp.exp(v[:, 1:2, :] - t_peak[None])
        total = lambda scale, n: jnp.sum(scale * v[:, n : n + 1, :], axis=0)
        s_tot, t_tot, cross = total(se, 2), total(te, 3), total(te, 4)
        kl_ref[...] = cross / t_tot - t_peak - jnp.log(t_tot) + s_peak + jnp.log(s_tot)
        c_ref[0:1, :] = s_peak
        c_ref[1:2, :] = t_peak
        c_ref[2:3, :] = w_ref[...] / s_tot
        c_ref[3:4, :] = w_ref[...] / t_tot

    es = jnp.exp(s_ref[...] - c_ref[0:1, :]) * c_ref[2:3, :]
    et = jnp.exp(t_ref[...].astype(F32) - c_ref[1:2, :]) * c_ref[3:4, :]
    g = (es - et).astype(BF16)
    at = step + cuts[0][0]
    for (first, steps), g_ref in zip(cuts, refs):

        @pl.when((at >= first) & (at < first + steps))
        def _():
            g_ref[...] = g


def piece(start, first, steps):
    return pl.BlockSpec((GB, T), lambda i: (jnp.clip(i + start - first, 0, steps - 1), 0))


def grad(gathered, w, s, t, cuts):
    start = cuts[0][0]
    block = pl.BlockSpec((GB, T), lambda i: (i + start, 0))
    return call(
        functools.partial(grad_body, cuts),
        out_shape=[jax.ShapeDtypeStruct((n * GB, T), BF16) for _, n in cuts] + [jax.ShapeDtypeStruct((1, T), F32)],
        grid=(sum(n for _, n in cuts),),
        in_specs=[whole((NV, 8, T)), whole((1, T)), block, block],
        out_specs=[piece(start, *cut) for cut in cuts] + [whole((1, T))],
        scratch_shapes=[pltpu.VMEM((8, T), F32)],
    )(gathered, w, s, t)


def hidden_body(pos, *refs):
    g_refs, (w_ref, mine_ref, other_ref, gt_ref) = refs[: len(CUTS)], refs[len(CUTS) :]

    @pl.when(pl.program_id(0) == 0)
    def _():
        for lo in range(0, VP, 128):
            rows = []
            for (first, steps), ref in zip(CUTS, g_refs):
                start, end = max(lo - first * GB, 0), min(lo + 128 - first * GB, steps * GB)
                if start < end:
                    rows.append(ref[start:end, :])
            x = jnp.concatenate(rows, axis=0)
            gt_ref[:, lo : lo + 128] = x.astype(F32).T.astype(BF16)

    p = jnp.dot(gt_ref[:, :VL], w_ref[...], preferred_element_type=F32).astype(BF16)
    even = pos[3] == 0
    for z in range(4):
        first, second = p[:, 256 * z : 256 * z + 128], p[:, 256 * z + 128 : 256 * z + 256]
        mine_ref[0, z] = jnp.where(even, first, second)
        other_ref[0, z] = jnp.where(even, second, first)


def hidden_part(pos, gs, wt):
    out = pl.BlockSpec((1, 4, T, 128), lambda i, p: (i, 0, 0, 0))
    return call(
        hidden_body,
        out_shape=[jax.ShapeDtypeStruct((4, 4, T, 128), BF16)] * 2,
        grid_spec=pltpu.PrefetchScalarGridSpec(
            num_scalar_prefetch=1,
            grid=(4,),
            in_specs=[whole(g.shape) for g in gs] + [pl.BlockSpec((VL, 1024), lambda i, p: (0, i))],
            out_specs=[out, out],
            scratch_shapes=[pltpu.VMEM((T, VP), BF16)],
        ),
    )(pos, *gs, wt)


def tokens_body(pos, h_ref, k_ref):
    for j in range(8):
        k_ref[:, j * 128 : (j + 1) * 128] = h_ref[j]


def tokens(pos, h2):
    group = lambda i, p: (p[0] + jnp.where(i == 0, 0, jnp.where(i == 1, 3, i - 1))) % 4
    return call(
        tokens_body,
        out_shape=jax.ShapeDtypeStruct((4 * T, DX), BF16),
        grid_spec=pltpu.PrefetchScalarGridSpec(
            num_scalar_prefetch=1,
            grid=(4,),
            in_specs=[pl.BlockSpec((8, T, 128), lambda i, p: (group(i, p), 0, 0))],
            out_specs=pl.BlockSpec((T, DX), lambda i, p: (i, 0)),
        ),
    )(pos, h2)


def head_body(near, far, prior, *refs):
    refs = list(refs)
    parts = [refs.pop(0)[...] for _ in range(3)] if near else []
    if far:
        far0, far1 = refs.pop(0), refs.pop(0)
        if far0.shape[0] < GB:
            parts.append(jnp.concatenate([far0[...], far1[...]], axis=0))
        else:
            parts.append(jnp.where(pl.program_id(0) == 0, far0[...], far1[...]))
    total = jnp.dot(jnp.concatenate(parts, axis=1), refs.pop(0)[...], preferred_element_type=F32)
    if prior:
        total = total + refs.pop(0)[...]
    refs[-1][...] = total.astype(refs[-1].dtype)


def head_piece(near, far, k, first, steps, prior=None, other=None):
    specs = [pl.BlockSpec((GB, T), lambda i: (i, 0))] * len(near) + [whole(g.shape) for g in far]
    rows = T * (len(near) + len(far) // 2)
    specs.append(pl.BlockSpec((rows, DX), lambda i: (0 if near else 3, 0)))
    args = [*near, *far, k]
    kw = {}
    if prior is not None:
        specs.append(pl.BlockSpec((GB, DX), lambda i: (i, 0)))
        args.append(prior)
    if other is not None:
        specs.append(pl.BlockSpec(memory_space=pl.ANY))
        args.append(other)
        kw["input_output_aliases"] = {len(args) - 1: 0}
    if far:
        out = jax.ShapeDtypeStruct((VL, DX), BF16)
    else:
        out, first = jax.ShapeDtypeStruct((steps * GB, DX), F32), 0
    return call(
        functools.partial(head_body, bool(near), bool(far), prior is not None),
        out_shape=out,
        grid=(steps,),
        in_specs=specs,
        out_specs=pl.BlockSpec((GB, DX), lambda i: (i + first, 0)),
        **kw,
    )(*args)


def shift(x, n):
    return lax.ppermute(x, "x", [(i, (i + n) % 4) for i in range(4)])


def swap(x):
    return lax.ppermute(x, "c", [(0, 1), (1, 0)])


def spread(x, first):
    got = [x]
    for n in (1, 2, 3):
        pairs = []
        for y in range(4):
            for z in range(4):
                for c in range(2):
                    to = (y, (z + n) % 4) if c == first else ((y + n) % 4, z)
                    pairs.append(((y * 4 + z) * 2 + c, (to[0] * 4 + to[1]) * 2 + c))
        got.append(lax.ppermute(x, V, pairs))
    return got


def after(x, *others):
    return lax.optimization_barrier((x,) + others)[0]


def per_device(hidden, head_weight, teacher_logits, row_weight):
    pos = jnp.stack([lax.axis_index(a) for a in ("x", "y", "z", "c")]).astype(jnp.int32)
    wt = head_weight.T
    blocks = prep(teacher_logits)
    one = jnp.stack(spread(hidden, 0))
    own = spread(after(one, blocks), 1)
    teacher = lax.all_to_all(after(blocks, *own[1:]), V, 0, 0, tiled=True)
    s, m, l = student(pos, wt, own, [swap(x) for x in own])
    t, share = stats(m, l, s, teacher)
    gathered = lax.all_to_all(share, V, 0, 0, tiled=True)

    w = row_weight.reshape(1, T)
    gu, kl = grad(gathered, w, s, t, CUTS[:1])
    gm, gl, _ = grad(gathered, after(w, gu), s, t, CUTS[1:])
    across = lax.ppermute(hidden, ("x", "y"), [(x * 4 + y, y * 4 + x) for x in range(4) for y in range(4)])
    h2 = lax.all_gather(after(across, kl), V)

    def near(g):
        return [g, shift(g, 1), shift(g, 3)]

    def far(parts, *first):
        half = parts[0].shape[0] // 2
        left, right = after(parts[1], *first), after(parts[2], *first)
        return [shift(left[:half], 1), shift(right[half:], 3)]

    near_u, near_m = near(gu), near(gm)
    far_u, far_m = far(near_u), far(near_m)
    near_l = near(after(gl, *far_u))
    mine, other = hidden_part(pos, (gu, gm, gl), wt)
    both = (mine.astype(F32) + swap(after(other, *near_u[1:], *near_m[1:])).astype(F32)).astype(BF16)
    both = after(both, *far_u)
    got = lax.all_to_all(both.reshape(16, T, 128), ("y", "z"), 0, 0, tiled=True)

    k = tokens(pos, h2)
    head = head_piece(near_u, far_u, k, *CUTS[0])
    head = head_piece(near_m, far_m, k, *CUTS[1], other=head)
    far_l = far(near_l, head)
    part = head_piece(near_l, [], k, *CUTS[2])
    grad_hidden = jnp.sum(after(got, part).astype(F32), axis=0).astype(BF16)
    head = head_piece([], far_l, k, *CUTS[2], prior=part, other=head)
    return kl.reshape(T), grad_hidden, head.T


def solution(mesh):
    fine = Mesh(mesh.devices.reshape(4, 4, 4, 2), ("x",) + V)
    in_specs = (P("x", V), P(None, V), P(("x",) + V, None), P("x"))
    out_specs = (P("x"), P("x", V), P("x", V))
    return jax.shard_map(per_device, mesh=fine, in_specs=in_specs, out_specs=out_specs, check_vma=False)
```

```python
import functools

import jax
import jax.numpy as jnp
from jax import lax
from jax.experimental import pallas as pl
from jax.experimental.pallas import tpu as pltpu
from jax.sharding import Mesh
from jax.sharding import PartitionSpec as P

F32, BF16 = jnp.float32, jnp.bfloat16
V = ("y", "z", "c")
NV = 32
VL = 2374
KT = 19
SB = 512
NS = 5
GB = 608
VP = 2432
CUTS = ((0, 2), (2, 1), (3, 1))
T = 512
D = 4096
DX = 1024
LOW = -1e30
MIB = 1 << 20


def call(body, **kw):
    return pl.pallas_call(
        body,
        compiler_params=pltpu.CompilerParams(vmem_limit_bytes=60 * MIB),
        cost_estimate=pl.CostEstimate(flops=1 << 20, bytes_accessed=1 << 16, transcendentals=0),
        **kw,
    )


def whole(shape):
    return pl.BlockSpec(shape, lambda *_: (0,) * len(shape))


def prep_body(t_ref, out_ref):
    end = NV * VL
    for i in range(NV):
        for k in range(KT):
            start = VL * i + 128 * k
            if start + 128 <= end:
                out_ref[i, k] = t_ref[:, start : start + 128]
            else:
                tile = t_ref[:, end - 128 : end].astype(F32)
                out_ref[i, k] = pltpu.roll(tile, end - start, axis=1).astype(BF16)


def prep(teacher):
    shape = (NV, KT, 16, 128)
    return call(
        prep_body,
        out_shape=jax.ShapeDtypeStruct(shape, BF16),
        grid=(1,),
        in_specs=[whole(teacher.shape)],
        out_specs=whole(shape),
    )(teacher)


def fold(x, op):
    return op(x.reshape(-1, 8, T), axis=0)


def student_body(pos, w_ref, *refs):
    own_refs, sib_refs, (s_ref, m_ref, l_ref, h_ref) = refs[:4], refs[4:8], refs[8:]
    step = pl.program_id(0)

    @pl.when(step == 0)
    def _():
        for a in range(4):
            for b in range(4):
                for ref, c in ((own_refs[a], pos[3]), (sib_refs[a], 1 - pos[3])):
                    y = (pos[1] + 4 - jnp.where(c == 0, a, b)) % 4
                    z = (pos[2] + 4 - jnp.where(c == 0, b, a)) % 4
                    at = pl.multiple_of(((y * 4 + z) * 2 + c) * 128, 128)
                    h_ref[:, pl.ds(at, 128)] = ref[b]
        m_ref[...] = jnp.full_like(m_ref, LOW)
        l_ref[...] = jnp.zeros_like(l_ref)

    s = lax.dot_general(w_ref[...], h_ref[...], (((1,), (1,)), ((), ())), preferred_element_type=F32)
    rows = step * SB + lax.broadcasted_iota(jnp.int32, s.shape, 0)
    s = jnp.where(rows < VL, s, LOW)
    s_ref[...] = s
    old = m_ref[...]
    peak = jnp.maximum(old, fold(s, jnp.max))
    m_ref[...] = peak
    es = jnp.exp(s.reshape(-1, 8, T) - peak[None])
    l_ref[...] = l_ref[...] * jnp.exp(old - peak) + jnp.sum(es, axis=0)


def student(pos, wt, own, sib):
    part = jax.ShapeDtypeStruct((8, T), F32)
    return call(
        student_body,
        out_shape=[jax.ShapeDtypeStruct((NS * SB, T), F32), part, part, jax.ShapeDtypeStruct((T, D), BF16)],
        grid_spec=pltpu.PrefetchScalarGridSpec(
            num_scalar_prefetch=1,
            grid=(NS,),
            in_specs=[pl.BlockSpec((SB, D), lambda i, p: (i, 0))] + [whole((4, T, 128))] * 8,
            out_specs=[pl.BlockSpec((SB, T), lambda i, p: (i, 0)), whole((8, T)), whole((8, T)), whole((T, D))],
        ),
    )(pos, wt, *own, *sib)


def stats_body(m_ref, l_ref, s_ref, t_ref, tt_ref, out_ref, p_ref, sum_ref, cross_ref):
    step = pl.program_id(0)

    @pl.when(step == 0)
    def _():
        p_ref[...] = jnp.full_like(p_ref, LOW)
        sum_ref[...] = jnp.zeros_like(sum_ref)
        cross_ref[...] = jnp.zeros_like(cross_ref)

    for n in range(SB // 128):

        @pl.when(step * (SB // 128) + n < KT)
        def _():
            t = t_ref[:, n].reshape(T, 128).T.astype(F32)
            rows = step * SB + n * 128 + lax.broadcasted_iota(jnp.int32, t.shape, 0)
            t = jnp.where(rows < VL, t, LOW)
            tt_ref[n * 128 : (n + 1) * 128, :] = t.astype(BF16)
            old = p_ref[...]
            peak = jnp.maximum(old, fold(t, jnp.max))
            p_ref[...] = peak
            scale = jnp.exp(old - peak)
            t = t.reshape(-1, 8, T)
            et = jnp.exp(t - peak[None])
            s = s_ref[n * 128 : (n + 1) * 128, :].reshape(-1, 8, T)
            sum_ref[...] = sum_ref[...] * scale + jnp.sum(et, axis=0)
            cross_ref[...] = cross_ref[...] * scale + jnp.sum(et * (t - s), axis=0)

    @pl.when(step == NS - 1)
    def _():
        s_peak = jnp.max(m_ref[...], axis=0, keepdims=True)
        t_peak = jnp.max(p_ref[...], axis=0, keepdims=True)
        se, te = jnp.exp(m_ref[...] - s_peak), jnp.exp(p_ref[...] - t_peak)
        total = lambda scale, ref: jnp.sum(scale * ref[...], axis=0, keepdims=True)
        values = [s_peak, t_peak, total(se, l_ref), total(te, sum_ref), total(te, cross_ref)]
        row = lax.broadcasted_iota(jnp.int32, (8, T), 0)
        out = jnp.zeros((8, T), F32)
        for n, v in enumerate(values):
            out = jnp.where(row == n, v, out)
        for i in range(NV):
            out_ref[i] = out


def stats(m, l, s, t):
    block = pl.BlockSpec((SB, T), lambda i: (i, 0))
    return call(
        stats_body,
        out_shape=[jax.ShapeDtypeStruct((NS * SB, T), BF16), jax.ShapeDtypeStruct((NV, 8, T), F32)],
        grid=(NS,),
        in_specs=[
            whole((8, T)),
            whole((8, T)),
            block,
            pl.BlockSpec((NV, SB // 128, 16, 128), lambda i: (0, i, 0, 0)),
        ],
        out_specs=[block, whole((NV, 8, T))],
        scratch_shapes=[pltpu.VMEM((8, T), F32)] * 3,
    )(m, l, s, t)


def grad_body(cuts, all_ref, w_ref, s_ref, t_ref, *refs):
    kl_ref, c_ref = refs[-2:]
    step = pl.program_id(0)

    @pl.when(step == 0)
    def _():
        v = all_ref[...]
        s_peak, t_peak = jnp.max(v[:, 0:1, :], axis=0), jnp.max(v[:, 1:2, :], axis=0)
        se, te = jnp.exp(v[:, 0:1, :] - s_peak[None]), jnp.exp(v[:, 1:2, :] - t_peak[None])
        total = lambda scale, n: jnp.sum(scale * v[:, n : n + 1, :], axis=0)
        s_tot, t_tot, cross = total(se, 2), total(te, 3), total(te, 4)
        kl_ref[...] = cross / t_tot - t_peak - jnp.log(t_tot) + s_peak + jnp.log(s_tot)
        c_ref[0:1, :] = s_peak
        c_ref[1:2, :] = t_peak
        c_ref[2:3, :] = w_ref[...] / s_tot
        c_ref[3:4, :] = w_ref[...] / t_tot

    es = jnp.exp(s_ref[...] - c_ref[0:1, :]) * c_ref[2:3, :]
    et = jnp.exp(t_ref[...].astype(F32) - c_ref[1:2, :]) * c_ref[3:4, :]
    g = (es - et).astype(BF16)
    at = step + cuts[0][0]
    for (first, steps), g_ref in zip(cuts, refs):

        @pl.when((at >= first) & (at < first + steps))
        def _():
            g_ref[...] = g


def piece(start, first, steps):
    return pl.BlockSpec((GB, T), lambda i: (jnp.clip(i + start - first, 0, steps - 1), 0))


def grad(gathered, w, s, t, cuts):
    start = cuts[0][0]
    block = pl.BlockSpec((GB, T), lambda i: (i + start, 0))
    return call(
        functools.partial(grad_body, cuts),
        out_shape=[jax.ShapeDtypeStruct((n * GB, T), BF16) for _, n in cuts] + [jax.ShapeDtypeStruct((1, T), F32)],
        grid=(sum(n for _, n in cuts),),
        in_specs=[whole((NV, 8, T)), whole((1, T)), block, block],
        out_specs=[piece(start, *cut) for cut in cuts] + [whole((1, T))],
        scratch_shapes=[pltpu.VMEM((8, T), F32)],
    )(gathered, w, s, t)


def hidden_body(pos, *refs):
    g_refs, (w_ref, mine_ref, other_ref, gt_ref) = refs[: len(CUTS)], refs[len(CUTS) :]

    @pl.when(pl.program_id(0) == 0)
    def _():
        for lo in range(0, VP, 128):
            rows = []
            for (first, steps), ref in zip(CUTS, g_refs):
                start, end = max(lo - first * GB, 0), min(lo + 128 - first * GB, steps * GB)
                if start < end:
                    rows.append(ref[start:end, :])
            x = jnp.concatenate(rows, axis=0)
            gt_ref[:, lo : lo + 128] = x.astype(F32).T.astype(BF16)

    p = jnp.dot(gt_ref[:, :VL], w_ref[...], preferred_element_type=F32).astype(BF16)
    even = pos[3] == 0
    for z in range(4):
        first, second = p[:, 256 * z : 256 * z + 128], p[:, 256 * z + 128 : 256 * z + 256]
        mine_ref[0, z] = jnp.where(even, first, second)
        other_ref[0, z] = jnp.where(even, second, first)


def hidden_part(pos, gs, wt):
    out = pl.BlockSpec((1, 4, T, 128), lambda i, p: (i, 0, 0, 0))
    return call(
        hidden_body,
        out_shape=[jax.ShapeDtypeStruct((4, 4, T, 128), BF16)] * 2,
        grid_spec=pltpu.PrefetchScalarGridSpec(
            num_scalar_prefetch=1,
            grid=(4,),
            in_specs=[whole(g.shape) for g in gs] + [pl.BlockSpec((VL, 1024), lambda i, p: (0, i))],
            out_specs=[out, out],
            scratch_shapes=[pltpu.VMEM((T, VP), BF16)],
        ),
    )(pos, *gs, wt)


def pick_body(pos, h_ref, *out_refs):
    for n, out_ref in enumerate(out_refs, 1):
        for z in range(4):
            at = pl.multiple_of((pos[0] + n) % 4 * DX + (2 * z + pos[3]) * 128, 128)
            out_ref[z] = h_ref[:, pl.ds(at, 128)]


def pick(pos, h):
    return call(
        pick_body,
        out_shape=[jax.ShapeDtypeStruct((4, T, 128), BF16)] * 3,
        grid_spec=pltpu.PrefetchScalarGridSpec(
            num_scalar_prefetch=1,
            grid=(1,),
            in_specs=[whole((T, D))],
            out_specs=[whole((4, T, 128))] * 3,
        ),
    )(pos, h)


def tokens_body(pos, h_ref, *refs):
    k_ref = refs[-1]
    k_ref[0:T, :] = h_ref[...]
    for n in range(3):
        rows = slice((n + 1) * T, (n + 2) * T)
        for ref, c in ((refs[2 * n], pos[3]), (refs[2 * n + 1], 1 - pos[3])):
            for z in range(4):
                k_ref[rows, pl.ds(pl.multiple_of((2 * z + c) * 128, 128), 128)] = ref[z]


def tokens(pos, h, parts):
    return call(
        tokens_body,
        out_shape=jax.ShapeDtypeStruct((4 * T, DX), BF16),
        grid_spec=pltpu.PrefetchScalarGridSpec(
            num_scalar_prefetch=1,
            grid=(1,),
            in_specs=[pl.BlockSpec((T, DX), lambda i, p: (0, p[0]))] + [whole((4, T, 128))] * 6,
            out_specs=whole((4 * T, DX)),
        ),
    )(pos, h, *parts)


def head_body(near, far, prior, *refs):
    refs = list(refs)
    parts = [refs.pop(0)[...] for _ in range(3)] if near else []
    if far:
        far0, far1 = refs.pop(0), refs.pop(0)
        if far0.shape[0] < GB:
            parts.append(jnp.concatenate([far0[...], far1[...]], axis=0))
        else:
            parts.append(jnp.where(pl.program_id(0) == 0, far0[...], far1[...]))
    total = jnp.dot(jnp.concatenate(parts, axis=1), refs.pop(0)[...], preferred_element_type=F32)
    if prior:
        total = total + refs.pop(0)[...]
    refs[-1][...] = total.astype(refs[-1].dtype)


def head_piece(near, far, k, first, steps, prior=None, other=None):
    specs = [pl.BlockSpec((GB, T), lambda i: (i, 0))] * len(near) + [whole(g.shape) for g in far]
    rows = T * (len(near) + len(far) // 2)
    specs.append(pl.BlockSpec((rows, DX), lambda i: (0 if near else 3, 0)))
    args = [*near, *far, k]
    kw = {}
    if prior is not None:
        specs.append(pl.BlockSpec((GB, DX), lambda i: (i, 0)))
        args.append(prior)
    if other is not None:
        specs.append(pl.BlockSpec(memory_space=pl.ANY))
        args.append(other)
        kw["input_output_aliases"] = {len(args) - 1: 0}
    if far:
        out = jax.ShapeDtypeStruct((VL, DX), BF16)
    else:
        out, first = jax.ShapeDtypeStruct((steps * GB, DX), F32), 0
    return call(
        functools.partial(head_body, bool(near), bool(far), prior is not None),
        out_shape=out,
        grid=(steps,),
        in_specs=specs,
        out_specs=pl.BlockSpec((GB, DX), lambda i: (i + first, 0)),
        **kw,
    )(*args)


def shift(x, n):
    return lax.ppermute(x, "x", [(i, (i + n) % 4) for i in range(4)])


def hop(x):
    return lax.ppermute(x, ("x", "c"), [(2 * i + c, (i + 1 + 2 * c) % 4 * 2 + c) for i in range(4) for c in range(2)])


def swap(x):
    return lax.ppermute(x, "c", [(0, 1), (1, 0)])


def spread(x, first):
    got = [x]
    for n in (1, 2, 3):
        pairs = []
        for y in range(4):
            for z in range(4):
                for c in range(2):
                    to = (y, (z + n) % 4) if c == first else ((y + n) % 4, z)
                    pairs.append(((y * 4 + z) * 2 + c, (to[0] * 4 + to[1]) * 2 + c))
        got.append(lax.ppermute(x, V, pairs))
    return got


def after(x, *others):
    return lax.optimization_barrier((x,) + others)[0]


def per_device(hidden, head_weight, teacher_logits, row_weight):
    pos = jnp.stack([lax.axis_index(a) for a in ("x", "y", "z", "c")]).astype(jnp.int32)
    wt = head_weight.T
    blocks = prep(teacher_logits)
    one = jnp.stack(spread(hidden, 0))
    own = spread(after(one, blocks), 1)
    teacher = lax.all_to_all(after(blocks, *own[1:]), V, 0, 0, tiled=True)
    s, m, l, h = student(pos, wt, own, [swap(x) for x in own])
    t, share = stats(m, l, s, teacher)
    gathered = lax.all_to_all(share, V, 0, 0, tiled=True)

    to_right, to_far, to_left = pick(pos, h)
    others = [shift(to_right, 1), shift(to_left, 3), hop(after(hop(to_far), share))]

    w = row_weight.reshape(1, T)
    gu, kl = grad(gathered, after(w, *others), s, t, CUTS[:1])
    gm, gl, _ = grad(gathered, after(w, gu), s, t, CUTS[1:])

    def near(g):
        return [g, shift(g, 1), shift(g, 3)]

    def far(parts, *first):
        half = parts[0].shape[0] // 2
        left, right = after(parts[1], *first), after(parts[2], *first)
        return [shift(left[:half], 1), shift(right[half:], 3)]

    near_u, near_m = near(gu), near(gm)
    far_u, far_m = far(near_u), far(near_m)
    near_l = near(after(gl, *far_u))
    mine, other = hidden_part(pos, (gu, gm, gl), wt)
    k = tokens(after(pos, mine), h, [x for other in others for x in (other, swap(other))])
    part_u = head_piece(near_u, [], k, *CUTS[0])
    both = (mine.astype(F32) + swap(after(other, *near_u[1:])).astype(F32)).astype(BF16)
    both = after(both, part_u, *near_m[1:])
    got = lax.all_to_all(both.reshape(16, T, 128), ("y", "z"), 0, 0, tiled=True)

    head = head_piece([], far_u, k, *CUTS[0], prior=part_u)
    head = head_piece(near_m, far_m, k, *CUTS[1], other=head)
    far_l = far(near_l, head)
    part_l = head_piece(near_l, [], k, *CUTS[2])
    grad_hidden = jnp.sum(after(got, part_l).astype(F32), axis=0).astype(BF16)
    head = head_piece([], far_l, k, *CUTS[2], prior=after(part_l, grad_hidden), other=head)
    return kl.reshape(T), grad_hidden, head.T


def solution(mesh):
    fine = Mesh(mesh.devices.reshape(4, 4, 4, 2), ("x",) + V)
    in_specs = (P("x", V), P(None, V), P(("x",) + V, None), P("x"))
    out_specs = (P("x"), P("x", V), P("x", V))
    return jax.shard_map(per_device, mesh=fine, in_specs=in_specs, out_specs=out_specs, check_vma=False)
```

```python
import functools

import jax
import jax.numpy as jnp
from jax import lax
from jax.experimental import pallas as pl
from jax.experimental.pallas import tpu as pltpu
from jax.sharding import Mesh
from jax.sharding import PartitionSpec as P

F32, BF16 = jnp.float32, jnp.bfloat16
V = ("y", "z", "c")
NV = 32
VL = 2374
KT = 19
SB = 512
NS = 5
GB = 608
VP = 2432
CUTS = ((0, 2), (2, 1), (3, 1))
T = 512
D = 4096
DX = 1024
LOW = -1e30
MIB = 1 << 20


def call(body, **kw):
    return pl.pallas_call(
        body,
        compiler_params=pltpu.CompilerParams(vmem_limit_bytes=60 * MIB),
        cost_estimate=pl.CostEstimate(flops=1 << 20, bytes_accessed=1 << 16, transcendentals=0),
        **kw,
    )


def whole(shape):
    return pl.BlockSpec(shape, lambda *_: (0,) * len(shape))


def prep_body(t_ref, out_ref):
    end = NV * VL
    for i in range(NV):
        for k in range(KT):
            start = VL * i + 128 * k
            if start + 128 <= end:
                out_ref[i, k] = t_ref[:, start : start + 128]
            else:
                tile = t_ref[:, end - 128 : end].astype(F32)
                out_ref[i, k] = pltpu.roll(tile, end - start, axis=1).astype(BF16)


def prep(teacher):
    shape = (NV, KT, 16, 128)
    return call(
        prep_body,
        out_shape=jax.ShapeDtypeStruct(shape, BF16),
        grid=(1,),
        in_specs=[whole(teacher.shape)],
        out_specs=whole(shape),
    )(teacher)


def fold(x, op):
    return op(x.reshape(-1, 8, T), axis=0)


def student_body(pos, w_ref, *refs):
    own_refs, sib_refs, (s_ref, m_ref, l_ref) = refs[:4], refs[4:8], refs[8:11]
    mine_ref, *next_refs, h_ref = refs[11:]
    step = pl.program_id(0)

    @pl.when(step == 0)
    def _():
        for a in range(4):
            for b in range(4):
                for ref, c in ((own_refs[a], pos[3]), (sib_refs[a], 1 - pos[3])):
                    y = (pos[1] + 4 - jnp.where(c == 0, a, b)) % 4
                    z = (pos[2] + 4 - jnp.where(c == 0, b, a)) % 4
                    at = pl.multiple_of(((y * 4 + z) * 2 + c) * 128, 128)
                    h_ref[:, pl.ds(at, 128)] = ref[b]
        mine_ref[...] = h_ref[:, pl.ds(pl.multiple_of(pos[0] * DX, 128), DX)]
        for n, out_ref in enumerate(next_refs, 1):
            for z in range(4):
                at = pl.multiple_of((pos[0] + n) % 4 * DX + (2 * z + pos[3]) * 128, 128)
                out_ref[z] = h_ref[:, pl.ds(at, 128)]
        m_ref[...] = jnp.full_like(m_ref, LOW)
        l_ref[...] = jnp.zeros_like(l_ref)

    s = lax.dot_general(w_ref[...], h_ref[...], (((1,), (1,)), ((), ())), preferred_element_type=F32)
    rows = step * SB + lax.broadcasted_iota(jnp.int32, s.shape, 0)
    s = jnp.where(rows < VL, s, LOW)
    s_ref[...] = s
    old = m_ref[...]
    peak = jnp.maximum(old, fold(s, jnp.max))
    m_ref[...] = peak
    es = jnp.exp(s.reshape(-1, 8, T) - peak[None])
    l_ref[...] = l_ref[...] * jnp.exp(old - peak) + jnp.sum(es, axis=0)


def student(pos, wt, own, sib):
    part = jax.ShapeDtypeStruct((8, T), F32)
    return call(
        student_body,
        out_shape=[
            jax.ShapeDtypeStruct((NS * SB, T), F32),
            part,
            part,
            jax.ShapeDtypeStruct((T, DX), BF16),
            *[jax.ShapeDtypeStruct((4, T, 128), BF16)] * 3,
        ],
        grid_spec=pltpu.PrefetchScalarGridSpec(
            num_scalar_prefetch=1,
            grid=(NS,),
            in_specs=[pl.BlockSpec((SB, D), lambda i, p: (i, 0))] + [whole((4, T, 128))] * 8,
            out_specs=[
                pl.BlockSpec((SB, T), lambda i, p: (i, 0)),
                whole((8, T)),
                whole((8, T)),
                whole((T, DX)),
                *[whole((4, T, 128))] * 3,
            ],
            scratch_shapes=[pltpu.VMEM((T, D), BF16)],
        ),
    )(pos, wt, *own, *sib)


def stats_body(m_ref, l_ref, s_ref, t_ref, tt_ref, out_ref, p_ref, sum_ref, cross_ref):
    step = pl.program_id(0)

    @pl.when(step == 0)
    def _():
        p_ref[...] = jnp.full_like(p_ref, LOW)
        sum_ref[...] = jnp.zeros_like(sum_ref)
        cross_ref[...] = jnp.zeros_like(cross_ref)

    for n in range(SB // 128):

        @pl.when(step * (SB // 128) + n < KT)
        def _():
            t = t_ref[:, n].reshape(T, 128).T.astype(F32)
            rows = step * SB + n * 128 + lax.broadcasted_iota(jnp.int32, t.shape, 0)
            t = jnp.where(rows < VL, t, LOW)
            tt_ref[n * 128 : (n + 1) * 128, :] = t.astype(BF16)
            old = p_ref[...]
            peak = jnp.maximum(old, fold(t, jnp.max))
            p_ref[...] = peak
            scale = jnp.exp(old - peak)
            t = t.reshape(-1, 8, T)
            et = jnp.exp(t - peak[None])
            s = s_ref[n * 128 : (n + 1) * 128, :].reshape(-1, 8, T)
            sum_ref[...] = sum_ref[...] * scale + jnp.sum(et, axis=0)
            cross_ref[...] = cross_ref[...] * scale + jnp.sum(et * (t - s), axis=0)

    @pl.when(step == NS - 1)
    def _():
        s_peak = jnp.max(m_ref[...], axis=0, keepdims=True)
        t_peak = jnp.max(p_ref[...], axis=0, keepdims=True)
        se, te = jnp.exp(m_ref[...] - s_peak), jnp.exp(p_ref[...] - t_peak)
        total = lambda scale, ref: jnp.sum(scale * ref[...], axis=0, keepdims=True)
        values = [s_peak, t_peak, total(se, l_ref), total(te, sum_ref), total(te, cross_ref)]
        row = lax.broadcasted_iota(jnp.int32, (8, T), 0)
        out = jnp.zeros((8, T), F32)
        for n, v in enumerate(values):
            out = jnp.where(row == n, v, out)
        for i in range(NV):
            out_ref[i] = out


def stats(m, l, s, t):
    block = pl.BlockSpec((SB, T), lambda i: (i, 0))
    return call(
        stats_body,
        out_shape=[jax.ShapeDtypeStruct((NS * SB, T), BF16), jax.ShapeDtypeStruct((NV, 8, T), F32)],
        grid=(NS,),
        in_specs=[
            whole((8, T)),
            whole((8, T)),
            block,
            pl.BlockSpec((NV, SB // 128, 16, 128), lambda i: (0, i, 0, 0)),
        ],
        out_specs=[block, whole((NV, 8, T))],
        scratch_shapes=[pltpu.VMEM((8, T), F32)] * 3,
    )(m, l, s, t)


def grad_body(cuts, all_ref, w_ref, s_ref, t_ref, *refs):
    kl_ref, c_ref = refs[-2:]
    step = pl.program_id(0)

    @pl.when(step == 0)
    def _():
        v = all_ref[...]
        s_peak, t_peak = jnp.max(v[:, 0:1, :], axis=0), jnp.max(v[:, 1:2, :], axis=0)
        se, te = jnp.exp(v[:, 0:1, :] - s_peak[None]), jnp.exp(v[:, 1:2, :] - t_peak[None])
        total = lambda scale, n: jnp.sum(scale * v[:, n : n + 1, :], axis=0)
        s_tot, t_tot, cross = total(se, 2), total(te, 3), total(te, 4)
        kl_ref[...] = cross / t_tot - t_peak - jnp.log(t_tot) + s_peak + jnp.log(s_tot)
        c_ref[0:1, :] = s_peak
        c_ref[1:2, :] = t_peak
        c_ref[2:3, :] = w_ref[...] / s_tot
        c_ref[3:4, :] = w_ref[...] / t_tot

    es = jnp.exp(s_ref[...] - c_ref[0:1, :]) * c_ref[2:3, :]
    et = jnp.exp(t_ref[...].astype(F32) - c_ref[1:2, :]) * c_ref[3:4, :]
    g = (es - et).astype(BF16)
    at = step + cuts[0][0]
    for (first, steps), g_ref in zip(cuts, refs):

        @pl.when((at >= first) & (at < first + steps))
        def _():
            g_ref[...] = g


def piece(start, first, steps):
    return pl.BlockSpec((GB, T), lambda i: (jnp.clip(i + start - first, 0, steps - 1), 0))


def grad(gathered, w, s, t, cuts):
    start = cuts[0][0]
    block = pl.BlockSpec((GB, T), lambda i: (i + start, 0))
    return call(
        functools.partial(grad_body, cuts),
        out_shape=[jax.ShapeDtypeStruct((n * GB, T), BF16) for _, n in cuts] + [jax.ShapeDtypeStruct((1, T), F32)],
        grid=(sum(n for _, n in cuts),),
        in_specs=[whole((NV, 8, T)), whole((1, T)), block, block],
        out_specs=[piece(start, *cut) for cut in cuts] + [whole((1, T))],
        scratch_shapes=[pltpu.VMEM((8, T), F32)],
    )(gathered, w, s, t)


def hidden_body(pos, *refs):
    g_refs, (w_ref, mine_ref, other_ref, gt_ref) = refs[: len(CUTS)], refs[len(CUTS) :]

    @pl.when(pl.program_id(0) == 0)
    def _():
        for lo in range(0, VP, 128):
            rows = []
            for (first, steps), ref in zip(CUTS, g_refs):
                start, end = max(lo - first * GB, 0), min(lo + 128 - first * GB, steps * GB)
                if start < end:
                    rows.append(ref[start:end, :])
            x = jnp.concatenate(rows, axis=0)
            gt_ref[:, lo : lo + 128] = x.astype(F32).T.astype(BF16)

    p = jnp.dot(gt_ref[:, :VL], w_ref[...], preferred_element_type=F32).astype(BF16)
    even = pos[3] == 0
    for z in range(4):
        first, second = p[:, 256 * z : 256 * z + 128], p[:, 256 * z + 128 : 256 * z + 256]
        mine_ref[0, z] = jnp.where(even, first, second)
        other_ref[0, z] = jnp.where(even, second, first)


def hidden_part(pos, gs, wt):
    out = pl.BlockSpec((1, 4, T, 128), lambda i, p: (i, 0, 0, 0))
    return call(
        hidden_body,
        out_shape=[jax.ShapeDtypeStruct((4, 4, T, 128), BF16)] * 2,
        grid_spec=pltpu.PrefetchScalarGridSpec(
            num_scalar_prefetch=1,
            grid=(4,),
            in_specs=[whole(g.shape) for g in gs] + [pl.BlockSpec((VL, 1024), lambda i, p: (0, i))],
            out_specs=[out, out],
            scratch_shapes=[pltpu.VMEM((T, VP), BF16)],
        ),
    )(pos, *gs, wt)


def tokens_body(pos, h_ref, *refs):
    k_ref = refs[-1]
    k_ref[0:T, :] = h_ref[...]
    for n in range(3):
        rows = slice((n + 1) * T, (n + 2) * T)
        for ref, c in ((refs[2 * n], pos[3]), (refs[2 * n + 1], 1 - pos[3])):
            for z in range(4):
                k_ref[rows, pl.ds(pl.multiple_of((2 * z + c) * 128, 128), 128)] = ref[z]


def tokens(pos, h, parts):
    return call(
        tokens_body,
        out_shape=jax.ShapeDtypeStruct((4 * T, DX), BF16),
        grid_spec=pltpu.PrefetchScalarGridSpec(
            num_scalar_prefetch=1,
            grid=(1,),
            in_specs=[whole((T, DX))] + [whole((4, T, 128))] * 6,
            out_specs=whole((4 * T, DX)),
        ),
    )(pos, h, *parts)


def head_body(near, far, prior, *refs):
    refs = list(refs)
    parts = [refs.pop(0)[...] for _ in range(3)] if near else []
    if far:
        far0, far1 = refs.pop(0), refs.pop(0)
        if far0.shape[0] < GB:
            parts.append(jnp.concatenate([far0[...], far1[...]], axis=0))
        else:
            parts.append(jnp.where(pl.program_id(0) == 0, far0[...], far1[...]))
    total = jnp.dot(jnp.concatenate(parts, axis=1), refs.pop(0)[...], preferred_element_type=F32)
    if prior:
        total = total + refs.pop(0)[...]
    refs[-1][...] = total.astype(refs[-1].dtype)


def head_piece(near, far, k, first, steps, prior=None, other=None):
    specs = [pl.BlockSpec((GB, T), lambda i: (i, 0))] * len(near) + [whole(g.shape) for g in far]
    rows = T * (len(near) + len(far) // 2)
    specs.append(pl.BlockSpec((rows, DX), lambda i: (0 if near else 3, 0)))
    args = [*near, *far, k]
    kw = {}
    if prior is not None:
        specs.append(pl.BlockSpec((GB, DX), lambda i: (i, 0)))
        args.append(prior)
    if other is not None:
        specs.append(pl.BlockSpec(memory_space=pl.ANY))
        args.append(other)
        kw["input_output_aliases"] = {len(args) - 1: 0}
    if far:
        out = jax.ShapeDtypeStruct((VL, DX), BF16)
    else:
        out, first = jax.ShapeDtypeStruct((steps * GB, DX), F32), 0
    return call(
        functools.partial(head_body, bool(near), bool(far), prior is not None),
        out_shape=out,
        grid=(steps,),
        in_specs=specs,
        out_specs=pl.BlockSpec((GB, DX), lambda i: (i + first, 0)),
        **kw,
    )(*args)


def head_all_body(pos, *refs):
    g = jnp.concatenate([r[0] for r in refs[:4]], axis=1)
    refs[-1][...] = jnp.dot(g, refs[4][...], preferred_element_type=F32).astype(BF16)


def head_all(pos, g, k, first, steps, other=None):
    specs = [
        pl.BlockSpec((1, GB, T), functools.partial(lambda away, i, p: ((p[0] + away) % 4, i, 0), away))
        for away in (0, 3, 1, 2)
    ]
    specs.append(whole((4 * T, DX)))
    args = [g] * 4 + [k]
    kw = {}
    if other is not None:
        specs.append(pl.BlockSpec(memory_space=pl.ANY))
        args.append(other)
        kw["input_output_aliases"] = {len(args): 0}
    return call(
        head_all_body,
        out_shape=jax.ShapeDtypeStruct((VL, DX), BF16),
        grid_spec=pltpu.PrefetchScalarGridSpec(
            num_scalar_prefetch=1,
            grid=(steps,),
            in_specs=specs,
            out_specs=pl.BlockSpec((GB, DX), lambda i, p: (i + first, 0)),
        ),
        **kw,
    )(pos, *args)


def shift(x, n):
    return lax.ppermute(x, "x", [(i, (i + n) % 4) for i in range(4)])


def hop(x):
    return lax.ppermute(x, ("x", "c"), [(2 * i + c, (i + 1 + 2 * c) % 4 * 2 + c) for i in range(4) for c in range(2)])


def swap(x):
    return lax.ppermute(x, "c", [(0, 1), (1, 0)])


def spread(x, first):
    got = [x]
    for n in (1, 2, 3):
        pairs = []
        for y in range(4):
            for z in range(4):
                for c in range(2):
                    to = (y, (z + n) % 4) if c == first else ((y + n) % 4, z)
                    pairs.append(((y * 4 + z) * 2 + c, (to[0] * 4 + to[1]) * 2 + c))
        got.append(lax.ppermute(x, V, pairs))
    return got


def after(x, *others):
    return lax.optimization_barrier((x,) + others)[0]


def per_device(hidden, head_weight, teacher_logits, row_weight):
    pos = jnp.stack([lax.axis_index(a) for a in ("x", "y", "z", "c")]).astype(jnp.int32)
    wt = head_weight.T
    blocks = prep(teacher_logits)
    one = jnp.stack(spread(hidden, 0))
    own = spread(after(one, blocks), 1)
    teacher = lax.all_to_all(after(blocks, *own[1:]), V, 0, 0, tiled=True)
    s, m, l, h, to_right, to_far, to_left = student(pos, wt, own, [swap(x) for x in own])
    t, share = stats(m, l, s, teacher)
    gathered = lax.all_to_all(share, V, 0, 0, tiled=True)

    others = [shift(to_right, 1), shift(to_left, 3), hop(after(hop(to_far), share))]

    w = row_weight.reshape(1, T)
    gu, kl = grad(gathered, after(w, *others), s, t, CUTS[:1])
    gm, gl, _ = grad(gathered, after(w, gu), s, t, CUTS[1:])

    def near(g):
        return [g, shift(g, 1), shift(g, 3)]

    def far(parts, *first):
        half = parts[0].shape[0] // 2
        left, right = after(parts[1], *first), after(parts[2], *first)
        return [shift(left[:half], 1), shift(right[half:], 3)]

    all_u, all_m = lax.all_gather(gu, "x"), lax.all_gather(gm, "x")
    near_l = near(gl)
    far_l = far(near_l)
    mine, other = hidden_part(pos, (gu, gm, gl), wt)
    k = tokens(after(pos, mine), h, [x for other in others for x in (other, swap(other))])
    both = (mine.astype(F32) + swap(after(other, *near_l[1:])).astype(F32)).astype(BF16)
    got = lax.all_to_all(both.reshape(16, T, 128), ("y", "z"), 0, 0, tiled=True)

    head = head_all(pos, all_u, k, *CUTS[0])
    head = head_piece(near_l, far_l, k, *CUTS[2], other=head)
    grad_hidden = jnp.sum(after(got, head).astype(F32), axis=0).astype(BF16)
    head = head_all(pos, all_m, k, *CUTS[1], other=head)
    return kl.reshape(T), grad_hidden, head.T


def solution(mesh):
    fine = Mesh(mesh.devices.reshape(4, 4, 4, 2), ("x",) + V)
    in_specs = (P("x", V), P(None, V), P(("x",) + V, None), P("x"))
    out_specs = (P("x"), P("x", V), P("x", V))
    return jax.shard_map(per_device, mesh=fine, in_specs=in_specs, out_specs=out_specs, check_vma=False)
```

```python
import functools

import jax
import jax.numpy as jnp
from jax import lax
from jax.experimental import pallas as pl
from jax.experimental.pallas import tpu as pltpu
from jax.sharding import Mesh
from jax.sharding import PartitionSpec as P

F32, BF16 = jnp.float32, jnp.bfloat16
V = ("y", "z", "c")
NV = 32
VL = 2374
KT = 19
SB = 512
NS = 5
GB = 608
VP = 2432
CUTS = ((0, 1), (1, 1), (2, 1), (3, 1))
T = 512
D = 4096
DX = 1024
LOW = -1e30
MIB = 1 << 20


def call(body, **kw):
    return pl.pallas_call(
        body,
        compiler_params=pltpu.CompilerParams(vmem_limit_bytes=60 * MIB),
        cost_estimate=pl.CostEstimate(flops=1 << 20, bytes_accessed=1 << 16, transcendentals=0),
        **kw,
    )


def whole(shape):
    return pl.BlockSpec(shape, lambda *_: (0,) * len(shape))


def prep_body(t_ref, out_ref):
    end = NV * VL
    for i in range(NV):
        for k in range(KT):
            start = VL * i + 128 * k
            if start + 128 <= end:
                out_ref[i, k] = t_ref[:, start : start + 128]
            else:
                tile = t_ref[:, end - 128 : end].astype(F32)
                out_ref[i, k] = pltpu.roll(tile, end - start, axis=1).astype(BF16)


def prep(teacher):
    shape = (NV, KT, 16, 128)
    return call(
        prep_body,
        out_shape=jax.ShapeDtypeStruct(shape, BF16),
        grid=(1,),
        in_specs=[whole(teacher.shape)],
        out_specs=whole(shape),
    )(teacher)


def fold(x, op):
    return op(x.reshape(-1, 8, T), axis=0)


def student_body(pos, w_ref, *refs):
    own_refs, sib_refs, (s_ref, m_ref, l_ref) = refs[:4], refs[4:8], refs[8:11]
    mine_ref, *next_refs, h_ref = refs[11:]
    step = pl.program_id(0)

    @pl.when(step == 0)
    def _():
        for a in range(4):
            for b in range(4):
                for ref, c in ((own_refs[a], pos[3]), (sib_refs[a], 1 - pos[3])):
                    y = (pos[1] + 4 - jnp.where(c == 0, a, b)) % 4
                    z = (pos[2] + 4 - jnp.where(c == 0, b, a)) % 4
                    at = pl.multiple_of(((y * 4 + z) * 2 + c) * 128, 128)
                    h_ref[:, pl.ds(at, 128)] = ref[b]
        mine_ref[...] = h_ref[:, pl.ds(pl.multiple_of(pos[0] * DX, 128), DX)]
        for n, out_ref in enumerate(next_refs, 1):
            for z in range(4):
                at = pl.multiple_of((pos[0] + n) % 4 * DX + (2 * z + pos[3]) * 128, 128)
                out_ref[z] = h_ref[:, pl.ds(at, 128)]
        m_ref[...] = jnp.full_like(m_ref, LOW)
        l_ref[...] = jnp.zeros_like(l_ref)

    s = lax.dot_general(w_ref[...], h_ref[...], (((1,), (1,)), ((), ())), preferred_element_type=F32)
    rows = step * SB + lax.broadcasted_iota(jnp.int32, s.shape, 0)
    s = jnp.where(rows < VL, s, LOW)
    s_ref[...] = s
    old = m_ref[...]
    peak = jnp.maximum(old, fold(s, jnp.max))
    m_ref[...] = peak
    es = jnp.exp(s.reshape(-1, 8, T) - peak[None])
    l_ref[...] = l_ref[...] * jnp.exp(old - peak) + jnp.sum(es, axis=0)


def student(pos, wt, own, sib):
    part = jax.ShapeDtypeStruct((8, T), F32)
    return call(
        student_body,
        out_shape=[
            jax.ShapeDtypeStruct((NS * SB, T), F32),
            part,
            part,
            jax.ShapeDtypeStruct((T, DX), BF16),
            *[jax.ShapeDtypeStruct((4, T, 128), BF16)] * 3,
        ],
        grid_spec=pltpu.PrefetchScalarGridSpec(
            num_scalar_prefetch=1,
            grid=(NS,),
            in_specs=[pl.BlockSpec((SB, D), lambda i, p: (i, 0))] + [whole((4, T, 128))] * 8,
            out_specs=[
                pl.BlockSpec((SB, T), lambda i, p: (i, 0)),
                whole((8, T)),
                whole((8, T)),
                whole((T, DX)),
                *[whole((4, T, 128))] * 3,
            ],
            scratch_shapes=[pltpu.VMEM((T, D), BF16)],
        ),
    )(pos, wt, *own, *sib)


def stats_body(m_ref, l_ref, s_ref, t_ref, tt_ref, out_ref, p_ref, sum_ref, cross_ref):
    step = pl.program_id(0)

    @pl.when(step == 0)
    def _():
        p_ref[...] = jnp.full_like(p_ref, LOW)
        sum_ref[...] = jnp.zeros_like(sum_ref)
        cross_ref[...] = jnp.zeros_like(cross_ref)

    for n in range(SB // 128):

        @pl.when(step * (SB // 128) + n < KT)
        def _():
            t = t_ref[:, n].reshape(T, 128).T.astype(F32)
            rows = step * SB + n * 128 + lax.broadcasted_iota(jnp.int32, t.shape, 0)
            t = jnp.where(rows < VL, t, LOW)
            tt_ref[n * 128 : (n + 1) * 128, :] = t.astype(BF16)
            old = p_ref[...]
            peak = jnp.maximum(old, fold(t, jnp.max))
            p_ref[...] = peak
            scale = jnp.exp(old - peak)
            t = t.reshape(-1, 8, T)
            et = jnp.exp(t - peak[None])
            s = s_ref[n * 128 : (n + 1) * 128, :].reshape(-1, 8, T)
            sum_ref[...] = sum_ref[...] * scale + jnp.sum(et, axis=0)
            cross_ref[...] = cross_ref[...] * scale + jnp.sum(et * (t - s), axis=0)

    @pl.when(step == NS - 1)
    def _():
        s_peak = jnp.max(m_ref[...], axis=0, keepdims=True)
        t_peak = jnp.max(p_ref[...], axis=0, keepdims=True)
        se, te = jnp.exp(m_ref[...] - s_peak), jnp.exp(p_ref[...] - t_peak)
        total = lambda scale, ref: jnp.sum(scale * ref[...], axis=0, keepdims=True)
        values = [s_peak, t_peak, total(se, l_ref), total(te, sum_ref), total(te, cross_ref)]
        row = lax.broadcasted_iota(jnp.int32, (8, T), 0)
        out = jnp.zeros((8, T), F32)
        for n, v in enumerate(values):
            out = jnp.where(row == n, v, out)
        for i in range(NV):
            out_ref[i] = out


def stats(m, l, s, t):
    block = pl.BlockSpec((SB, T), lambda i: (i, 0))
    return call(
        stats_body,
        out_shape=[jax.ShapeDtypeStruct((NS * SB, T), BF16), jax.ShapeDtypeStruct((NV, 8, T), F32)],
        grid=(NS,),
        in_specs=[
            whole((8, T)),
            whole((8, T)),
            block,
            pl.BlockSpec((NV, SB // 128, 16, 128), lambda i: (0, i, 0, 0)),
        ],
        out_specs=[block, whole((NV, 8, T))],
        scratch_shapes=[pltpu.VMEM((8, T), F32)] * 3,
    )(m, l, s, t)


def grad_body(cuts, all_ref, w_ref, s_ref, t_ref, *refs):
    kl_ref, c_ref = refs[-2:]
    step = pl.program_id(0)

    @pl.when(step == 0)
    def _():
        v = all_ref[...]
        s_peak, t_peak = jnp.max(v[:, 0:1, :], axis=0), jnp.max(v[:, 1:2, :], axis=0)
        se, te = jnp.exp(v[:, 0:1, :] - s_peak[None]), jnp.exp(v[:, 1:2, :] - t_peak[None])
        total = lambda scale, n: jnp.sum(scale * v[:, n : n + 1, :], axis=0)
        s_tot, t_tot, cross = total(se, 2), total(te, 3), total(te, 4)
        kl_ref[...] = cross / t_tot - t_peak - jnp.log(t_tot) + s_peak + jnp.log(s_tot)
        c_ref[0:1, :] = s_peak
        c_ref[1:2, :] = t_peak
        c_ref[2:3, :] = w_ref[...] / s_tot
        c_ref[3:4, :] = w_ref[...] / t_tot

    es = jnp.exp(s_ref[...] - c_ref[0:1, :]) * c_ref[2:3, :]
    et = jnp.exp(t_ref[...].astype(F32) - c_ref[1:2, :]) * c_ref[3:4, :]
    g = (es - et).astype(BF16)
    at = step + cuts[0][0]
    for (first, steps), g_ref in zip(cuts, refs):

        @pl.when((at >= first) & (at < first + steps))
        def _():
            g_ref[...] = g


def piece(start, first, steps):
    return pl.BlockSpec((GB, T), lambda i: (jnp.clip(i + start - first, 0, steps - 1), 0))


def grad(gathered, w, s, t, cuts):
    start = cuts[0][0]
    block = pl.BlockSpec((GB, T), lambda i: (i + start, 0))
    return call(
        functools.partial(grad_body, cuts),
        out_shape=[jax.ShapeDtypeStruct((n * GB, T), BF16) for _, n in cuts] + [jax.ShapeDtypeStruct((1, T), F32)],
        grid=(sum(n for _, n in cuts),),
        in_specs=[whole((NV, 8, T)), whole((1, T)), block, block],
        out_specs=[piece(start, *cut) for cut in cuts] + [whole((1, T))],
        scratch_shapes=[pltpu.VMEM((8, T), F32)],
    )(gathered, w, s, t)


def hidden_body(pos, *refs):
    g_refs, (w_ref, mine_ref, other_ref, gt_ref) = refs[: len(CUTS)], refs[len(CUTS) :]

    @pl.when(pl.program_id(0) == 0)
    def _():
        for lo in range(0, VP, 128):
            rows = []
            for (first, steps), ref in zip(CUTS, g_refs):
                start, end = max(lo - first * GB, 0), min(lo + 128 - first * GB, steps * GB)
                if start < end:
                    rows.append(ref[start:end, :])
            x = jnp.concatenate(rows, axis=0)
            gt_ref[:, lo : lo + 128] = x.astype(F32).T.astype(BF16)

    p = jnp.dot(gt_ref[:, :VL], w_ref[...], preferred_element_type=F32).astype(BF16)
    even = pos[3] == 0
    for z in range(4):
        first, second = p[:, 256 * z : 256 * z + 128], p[:, 256 * z + 128 : 256 * z + 256]
        mine_ref[0, z] = jnp.where(even, first, second)
        other_ref[0, z] = jnp.where(even, second, first)


def hidden_part(pos, gs, wt):
    out = pl.BlockSpec((1, 4, T, 128), lambda i, p: (i, 0, 0, 0))
    return call(
        hidden_body,
        out_shape=[jax.ShapeDtypeStruct((4, 4, T, 128), BF16)] * 2,
        grid_spec=pltpu.PrefetchScalarGridSpec(
            num_scalar_prefetch=1,
            grid=(4,),
            in_specs=[whole(g.shape) for g in gs] + [pl.BlockSpec((VL, 1024), lambda i, p: (0, i))],
            out_specs=[out, out],
            scratch_shapes=[pltpu.VMEM((T, VP), BF16)],
        ),
    )(pos, *gs, wt)


def tokens_body(pos, h_ref, *refs):
    k_ref = refs[-1]
    k_ref[0:T, :] = h_ref[...]
    for n in range(3):
        rows = slice((n + 1) * T, (n + 2) * T)
        for ref, c in ((refs[2 * n], pos[3]), (refs[2 * n + 1], 1 - pos[3])):
            for z in range(4):
                k_ref[rows, pl.ds(pl.multiple_of((2 * z + c) * 128, 128), 128)] = ref[z]


def tokens(pos, h, parts):
    return call(
        tokens_body,
        out_shape=jax.ShapeDtypeStruct((4 * T, DX), BF16),
        grid_spec=pltpu.PrefetchScalarGridSpec(
            num_scalar_prefetch=1,
            grid=(1,),
            in_specs=[whole((T, DX))] + [whole((4, T, 128))] * 6,
            out_specs=whole((4 * T, DX)),
        ),
    )(pos, h, *parts)


def head_body(near, far, prior, *refs):
    refs = list(refs)
    parts = [refs.pop(0)[...] for _ in range(3)] if near else []
    if far:
        far0, far1 = refs.pop(0), refs.pop(0)
        if far0.shape[0] < GB:
            parts.append(jnp.concatenate([far0[...], far1[...]], axis=0))
        else:
            parts.append(jnp.where(pl.program_id(0) == 0, far0[...], far1[...]))
    total = jnp.dot(jnp.concatenate(parts, axis=1), refs.pop(0)[...], preferred_element_type=F32)
    if prior:
        total = total + refs.pop(0)[...]
    refs[-1][...] = total.astype(refs[-1].dtype)


def head_piece(near, far, k, first, steps, prior=None, other=None):
    specs = [pl.BlockSpec((GB, T), lambda i: (i, 0))] * len(near) + [whole(g.shape) for g in far]
    rows = T * (len(near) + len(far) // 2)
    specs.append(pl.BlockSpec((rows, DX), lambda i: (0 if near else 3, 0)))
    args = [*near, *far, k]
    kw = {}
    if prior is not None:
        specs.append(pl.BlockSpec((GB, DX), lambda i: (i, 0)))
        args.append(prior)
    if other is not None:
        specs.append(pl.BlockSpec(memory_space=pl.ANY))
        args.append(other)
        kw["input_output_aliases"] = {len(args) - 1: 0}
    if far:
        out = jax.ShapeDtypeStruct((VL, DX), BF16)
    else:
        out, first = jax.ShapeDtypeStruct((steps * GB, DX), F32), 0
    return call(
        functools.partial(head_body, bool(near), bool(far), prior is not None),
        out_shape=out,
        grid=(steps,),
        in_specs=specs,
        out_specs=pl.BlockSpec((GB, DX), lambda i: (i + first, 0)),
        **kw,
    )(*args)


def head_all_body(pos, *refs):
    g = jnp.concatenate([r[0] for r in refs[:4]], axis=1)
    refs[-1][...] = jnp.dot(g, refs[4][...], preferred_element_type=F32).astype(BF16)


def head_all(pos, g, k, first, steps, other=None):
    specs = [
        pl.BlockSpec((1, GB, T), functools.partial(lambda away, i, p: ((p[0] + away) % 4, i, 0), away))
        for away in (0, 3, 1, 2)
    ]
    specs.append(whole((4 * T, DX)))
    args = [g] * 4 + [k]
    kw = {}
    if other is not None:
        specs.append(pl.BlockSpec(memory_space=pl.ANY))
        args.append(other)
        kw["input_output_aliases"] = {len(args): 0}
    return call(
        head_all_body,
        out_shape=jax.ShapeDtypeStruct((VL, DX), BF16),
        grid_spec=pltpu.PrefetchScalarGridSpec(
            num_scalar_prefetch=1,
            grid=(steps,),
            in_specs=specs,
            out_specs=pl.BlockSpec((GB, DX), lambda i, p: (i + first, 0)),
        ),
        **kw,
    )(pos, *args)


def shift(x, n):
    return lax.ppermute(x, "x", [(i, (i + n) % 4) for i in range(4)])


def hop(x):
    return lax.ppermute(x, ("x", "c"), [(2 * i + c, (i + 1 + 2 * c) % 4 * 2 + c) for i in range(4) for c in range(2)])


def swap(x):
    return lax.ppermute(x, "c", [(0, 1), (1, 0)])


def spread(x, first):
    got = [x]
    for n in (1, 2, 3):
        pairs = []
        for y in range(4):
            for z in range(4):
                for c in range(2):
                    to = (y, (z + n) % 4) if c == first else ((y + n) % 4, z)
                    pairs.append(((y * 4 + z) * 2 + c, (to[0] * 4 + to[1]) * 2 + c))
        got.append(lax.ppermute(x, V, pairs))
    return got


def after(x, *others):
    return lax.optimization_barrier((x,) + others)[0]


def per_device(hidden, head_weight, teacher_logits, row_weight):
    pos = jnp.stack([lax.axis_index(a) for a in ("x", "y", "z", "c")]).astype(jnp.int32)
    wt = head_weight.T
    blocks = prep(teacher_logits)
    one = jnp.stack(spread(hidden, 0))
    own = spread(after(one, blocks), 1)
    teacher = lax.all_to_all(after(blocks, *own[1:]), V, 0, 0, tiled=True)
    s, m, l, h, to_right, to_far, to_left = student(pos, wt, own, [swap(x) for x in own])
    t, share = stats(m, l, s, teacher)
    gathered = lax.all_to_all(share, V, 0, 0, tiled=True)

    others = [shift(to_right, 1), shift(to_left, 3), hop(after(hop(to_far), share))]

    w = row_weight.reshape(1, T)
    g0, kl = grad(gathered, after(w, *others), s, t, CUTS[:1])
    g1, g2, g3, _ = grad(gathered, after(w, g0), s, t, CUTS[1:])

    def near(g):
        return [g, shift(g, 1), shift(g, 3)]

    def far(parts, *first):
        half = parts[0].shape[0] // 2
        left, right = after(parts[1], *first), after(parts[2], *first)
        return [shift(left[:half], 1), shift(right[half:], 3)]

    all0, all1 = lax.all_gather(g0, "x"), lax.all_gather(g1, "x")
    near2 = near(g2)
    near3 = near(after(g3, *near2[1:]))
    mine, other = hidden_part(pos, (g0, g1, g2, g3), wt)
    others = [x for other in others for x in (other, swap(after(other, gathered)))]
    k = tokens(after(pos, mine), h, others)
    both = (mine.astype(F32) + swap(after(other, k, *near2[1:])).astype(F32)).astype(BF16)
    got = lax.all_to_all(both.reshape(16, T, 128), ("y", "z"), 0, 0, tiled=True)

    head = head_all(pos, all0, k, *CUTS[0])
    far2, far3 = far(near2, head), far(near3, head)
    head = head_piece(near2, far2, k, *CUTS[2], other=head)
    head = head_piece(near3, far3, k, *CUTS[3], other=head)
    grad_hidden = jnp.sum(after(got, head).astype(F32), axis=0).astype(BF16)
    head = head_all(pos, all1, k, *CUTS[1], other=head)
    return kl.reshape(T), grad_hidden, head.T


def solution(mesh):
    fine = Mesh(mesh.devices.reshape(4, 4, 4, 2), ("x",) + V)
    in_specs = (P("x", V), P(None, V), P(("x",) + V, None), P("x"))
    out_specs = (P("x"), P("x", V), P("x", V))
    return jax.shard_map(per_device, mesh=fine, in_specs=in_specs, out_specs=out_specs, check_vma=False)
```

```python
import functools

import jax
import jax.numpy as jnp
from jax import lax
from jax.experimental import pallas as pl
from jax.experimental.pallas import tpu as pltpu
from jax.sharding import Mesh
from jax.sharding import PartitionSpec as P

F32, BF16 = jnp.float32, jnp.bfloat16
V = ("y", "z", "c")
NV = 32
VL = 2374
KT = 19
SB = 512
NS = 5
GB = 304
VP = 2432
CUTS = ((0, 4), (4, 1), (5, 3))
T = 512
D = 4096
DX = 1024
LOW = -1e30
MIB = 1 << 20


def call(body, **kw):
    return pl.pallas_call(
        body,
        compiler_params=pltpu.CompilerParams(vmem_limit_bytes=60 * MIB),
        cost_estimate=pl.CostEstimate(flops=1 << 20, bytes_accessed=1 << 16, transcendentals=0),
        **kw,
    )


def whole(shape):
    return pl.BlockSpec(shape, lambda *_: (0,) * len(shape))


def prep_body(t_ref, out_ref):
    end = NV * VL
    for i in range(NV):
        for k in range(KT):
            start = VL * i + 128 * k
            if start + 128 <= end:
                out_ref[i, k] = t_ref[:, start : start + 128]
            else:
                tile = t_ref[:, end - 128 : end].astype(F32)
                out_ref[i, k] = pltpu.roll(tile, end - start, axis=1).astype(BF16)


def prep(teacher):
    shape = (NV, KT, 16, 128)
    return call(
        prep_body,
        out_shape=jax.ShapeDtypeStruct(shape, BF16),
        grid=(1,),
        in_specs=[whole(teacher.shape)],
        out_specs=whole(shape),
    )(teacher)


def fold(x, op):
    return op(x.reshape(-1, 8, T), axis=0)


def student_body(pos, w_ref, *refs):
    own_refs, sib_refs, (s_ref, m_ref, l_ref) = refs[:4], refs[4:8], refs[8:11]
    mine_ref, *next_refs, h_ref = refs[11:]
    step = pl.program_id(0)

    @pl.when(step == 0)
    def _():
        for a in range(4):
            for b in range(4):
                for ref, c in ((own_refs[a], pos[3]), (sib_refs[a], 1 - pos[3])):
                    y = (pos[1] + 4 - jnp.where(c == 0, a, b)) % 4
                    z = (pos[2] + 4 - jnp.where(c == 0, b, a)) % 4
                    at = pl.multiple_of(((y * 4 + z) * 2 + c) * 128, 128)
                    h_ref[:, pl.ds(at, 128)] = ref[b]
        mine_ref[...] = h_ref[:, pl.ds(pl.multiple_of(pos[0] * DX, 128), DX)]
        for n, out_ref in enumerate(next_refs, 1):
            for z in range(4):
                at = pl.multiple_of((pos[0] + n) % 4 * DX + (2 * z + pos[3]) * 128, 128)
                out_ref[z] = h_ref[:, pl.ds(at, 128)]
        m_ref[...] = jnp.full_like(m_ref, LOW)
        l_ref[...] = jnp.zeros_like(l_ref)

    s = lax.dot_general(w_ref[...], h_ref[...], (((1,), (1,)), ((), ())), preferred_element_type=F32)
    rows = step * SB + lax.broadcasted_iota(jnp.int32, s.shape, 0)
    s = jnp.where(rows < VL, s, LOW)
    s_ref[...] = s
    old = m_ref[...]
    peak = jnp.maximum(old, fold(s, jnp.max))
    m_ref[...] = peak
    es = jnp.exp(s.reshape(-1, 8, T) - peak[None])
    l_ref[...] = l_ref[...] * jnp.exp(old - peak) + jnp.sum(es, axis=0)


def student(pos, wt, own, sib):
    part = jax.ShapeDtypeStruct((8, T), F32)
    return call(
        student_body,
        out_shape=[
            jax.ShapeDtypeStruct((NS * SB, T), F32),
            part,
            part,
            jax.ShapeDtypeStruct((T, DX), BF16),
            *[jax.ShapeDtypeStruct((4, T, 128), BF16)] * 3,
        ],
        grid_spec=pltpu.PrefetchScalarGridSpec(
            num_scalar_prefetch=1,
            grid=(NS,),
            in_specs=[pl.BlockSpec((SB, D), lambda i, p: (i, 0))] + [whole((4, T, 128))] * 8,
            out_specs=[
                pl.BlockSpec((SB, T), lambda i, p: (i, 0)),
                whole((8, T)),
                whole((8, T)),
                whole((T, DX)),
                *[whole((4, T, 128))] * 3,
            ],
            scratch_shapes=[pltpu.VMEM((T, D), BF16)],
        ),
    )(pos, wt, *own, *sib)


def stats_body(m_ref, l_ref, s_ref, t_ref, tt_ref, out_ref, p_ref, sum_ref, cross_ref):
    step = pl.program_id(0)

    @pl.when(step == 0)
    def _():
        p_ref[...] = jnp.full_like(p_ref, LOW)
        sum_ref[...] = jnp.zeros_like(sum_ref)
        cross_ref[...] = jnp.zeros_like(cross_ref)

    for n in range(SB // 128):

        @pl.when(step * (SB // 128) + n < KT)
        def _():
            t = t_ref[:, n].reshape(T, 128).T.astype(F32)
            rows = step * SB + n * 128 + lax.broadcasted_iota(jnp.int32, t.shape, 0)
            t = jnp.where(rows < VL, t, LOW)
            tt_ref[n * 128 : (n + 1) * 128, :] = t.astype(BF16)
            old = p_ref[...]
            peak = jnp.maximum(old, fold(t, jnp.max))
            p_ref[...] = peak
            scale = jnp.exp(old - peak)
            t = t.reshape(-1, 8, T)
            et = jnp.exp(t - peak[None])
            s = s_ref[n * 128 : (n + 1) * 128, :].reshape(-1, 8, T)
            sum_ref[...] = sum_ref[...] * scale + jnp.sum(et, axis=0)
            cross_ref[...] = cross_ref[...] * scale + jnp.sum(et * (t - s), axis=0)

    @pl.when(step == NS - 1)
    def _():
        s_peak = jnp.max(m_ref[...], axis=0, keepdims=True)
        t_peak = jnp.max(p_ref[...], axis=0, keepdims=True)
        se, te = jnp.exp(m_ref[...] - s_peak), jnp.exp(p_ref[...] - t_peak)
        total = lambda scale, ref: jnp.sum(scale * ref[...], axis=0, keepdims=True)
        values = [s_peak, t_peak, total(se, l_ref), total(te, sum_ref), total(te, cross_ref)]
        row = lax.broadcasted_iota(jnp.int32, (8, T), 0)
        out = jnp.zeros((8, T), F32)
        for n, v in enumerate(values):
            out = jnp.where(row == n, v, out)
        for i in range(NV):
            out_ref[i] = out


def stats(m, l, s, t):
    block = pl.BlockSpec((SB, T), lambda i: (i, 0))
    return call(
        stats_body,
        out_shape=[jax.ShapeDtypeStruct((NS * SB, T), BF16), jax.ShapeDtypeStruct((NV, 8, T), F32)],
        grid=(NS,),
        in_specs=[
            whole((8, T)),
            whole((8, T)),
            block,
            pl.BlockSpec((NV, SB // 128, 16, 128), lambda i: (0, i, 0, 0)),
        ],
        out_specs=[block, whole((NV, 8, T))],
        scratch_shapes=[pltpu.VMEM((8, T), F32)] * 3,
    )(m, l, s, t)


def grad_body(cuts, all_ref, w_ref, s_ref, t_ref, *refs):
    kl_ref, c_ref = refs[-2:]
    step = pl.program_id(0)

    @pl.when(step == 0)
    def _():
        v = all_ref[...]
        s_peak, t_peak = jnp.max(v[:, 0:1, :], axis=0), jnp.max(v[:, 1:2, :], axis=0)
        se, te = jnp.exp(v[:, 0:1, :] - s_peak[None]), jnp.exp(v[:, 1:2, :] - t_peak[None])
        total = lambda scale, n: jnp.sum(scale * v[:, n : n + 1, :], axis=0)
        s_tot, t_tot, cross = total(se, 2), total(te, 3), total(te, 4)
        kl_ref[...] = cross / t_tot - t_peak - jnp.log(t_tot) + s_peak + jnp.log(s_tot)
        c_ref[0:1, :] = s_peak
        c_ref[1:2, :] = t_peak
        c_ref[2:3, :] = w_ref[...] / s_tot
        c_ref[3:4, :] = w_ref[...] / t_tot

    es = jnp.exp(s_ref[...] - c_ref[0:1, :]) * c_ref[2:3, :]
    et = jnp.exp(t_ref[...].astype(F32) - c_ref[1:2, :]) * c_ref[3:4, :]
    g = (es - et).astype(BF16)
    at = step + cuts[0][0]
    for (first, steps), g_ref in zip(cuts, refs):

        @pl.when((at >= first) & (at < first + steps))
        def _():
            g_ref[...] = g


def piece(start, first, steps):
    return pl.BlockSpec((GB, T), lambda i: (jnp.clip(i + start - first, 0, steps - 1), 0))


def grad(gathered, w, s, t, cuts):
    start = cuts[0][0]
    block = pl.BlockSpec((GB, T), lambda i: (i + start, 0))
    return call(
        functools.partial(grad_body, cuts),
        out_shape=[jax.ShapeDtypeStruct((n * GB, T), BF16) for _, n in cuts] + [jax.ShapeDtypeStruct((1, T), F32)],
        grid=(sum(n for _, n in cuts),),
        in_specs=[whole((NV, 8, T)), whole((1, T)), block, block],
        out_specs=[piece(start, *cut) for cut in cuts] + [whole((1, T))],
        scratch_shapes=[pltpu.VMEM((8, T), F32)],
    )(gathered, w, s, t)


def hidden_body(pos, *refs):
    g_refs, (w_ref, mine_ref, other_ref, gt_ref) = refs[: len(CUTS)], refs[len(CUTS) :]

    @pl.when(pl.program_id(0) == 0)
    def _():
        for lo in range(0, VP, 128):
            rows = []
            for (first, steps), ref in zip(CUTS, g_refs):
                start, end = max(lo - first * GB, 0), min(lo + 128 - first * GB, steps * GB)
                if start < end:
                    rows.append(ref[start:end, :])
            x = jnp.concatenate(rows, axis=0)
            gt_ref[:, lo : lo + 128] = x.astype(F32).T.astype(BF16)

    p = jnp.dot(gt_ref[:, :VL], w_ref[...], preferred_element_type=F32).astype(BF16)
    even = pos[3] == 0
    for z in range(4):
        first, second = p[:, 256 * z : 256 * z + 128], p[:, 256 * z + 128 : 256 * z + 256]
        mine_ref[0, z] = jnp.where(even, first, second)
        other_ref[0, z] = jnp.where(even, second, first)


def hidden_part(pos, gs, wt):
    out = pl.BlockSpec((1, 4, T, 128), lambda i, p: (i, 0, 0, 0))
    return call(
        hidden_body,
        out_shape=[jax.ShapeDtypeStruct((4, 4, T, 128), BF16)] * 2,
        grid_spec=pltpu.PrefetchScalarGridSpec(
            num_scalar_prefetch=1,
            grid=(4,),
            in_specs=[whole(g.shape) for g in gs] + [pl.BlockSpec((VL, 1024), lambda i, p: (0, i))],
            out_specs=[out, out],
            scratch_shapes=[pltpu.VMEM((T, VP), BF16)],
        ),
    )(pos, *gs, wt)


def tokens_body(pos, h_ref, *refs):
    k_ref = refs[-1]
    k_ref[0:T, :] = h_ref[...]
    for n in range(3):
        rows = slice((n + 1) * T, (n + 2) * T)
        for ref, c in ((refs[2 * n], pos[3]), (refs[2 * n + 1], 1 - pos[3])):
            for z in range(4):
                k_ref[rows, pl.ds(pl.multiple_of((2 * z + c) * 128, 128), 128)] = ref[z]


def tokens(pos, h, parts):
    return call(
        tokens_body,
        out_shape=jax.ShapeDtypeStruct((4 * T, DX), BF16),
        grid_spec=pltpu.PrefetchScalarGridSpec(
            num_scalar_prefetch=1,
            grid=(1,),
            in_specs=[whole((T, DX))] + [whole((4, T, 128))] * 6,
            out_specs=whole((4 * T, DX)),
        ),
    )(pos, h, *parts)


def head_body(pos, *refs):
    g = jnp.concatenate([r[...].reshape(-1, T) for r in refs[:4]], axis=1)
    refs[-1][...] = jnp.dot(g, refs[4][...], preferred_element_type=F32).astype(BF16)


def head_rows(pos, gs, k, first, steps, other=None):
    if len(gs) == 1:
        rows = GB * 2 if steps % 2 == 0 else GB
        specs = [
            pl.BlockSpec((1, rows, T), functools.partial(lambda away, i, p: ((p[0] + away) % 4, i, 0), away))
            for away in (0, 3, 1, 2)
        ]
    else:
        rows = GB
        specs = [pl.BlockSpec((rows, T), lambda i, p: (i, 0))] * 4
    start = first * GB // rows
    specs.append(whole((4 * T, DX)))
    args = [*(gs * 4 if len(gs) == 1 else gs), k]
    kw = {}
    if other is not None:
        specs.append(pl.BlockSpec(memory_space=pl.ANY))
        args.append(other)
        kw["input_output_aliases"] = {len(args): 0}
    return call(
        head_body,
        out_shape=jax.ShapeDtypeStruct((VL, DX), BF16),
        grid_spec=pltpu.PrefetchScalarGridSpec(
            num_scalar_prefetch=1,
            grid=(steps * GB // rows,),
            in_specs=specs,
            out_specs=pl.BlockSpec((rows, DX), lambda i, p: (i + start, 0)),
        ),
        **kw,
    )(pos, *args)


def shift(x, n):
    return lax.ppermute(x, "x", [(i, (i + n) % 4) for i in range(4)])


def hop(x):
    return lax.ppermute(x, ("x", "c"), [(2 * i + c, (i + 1 + 2 * c) % 4 * 2 + c) for i in range(4) for c in range(2)])


def swap(x):
    return lax.ppermute(x, "c", [(0, 1), (1, 0)])


def spread(x, first):
    got = [x]
    for n in (1, 2, 3):
        pairs = []
        for y in range(4):
            for z in range(4):
                for c in range(2):
                    to = (y, (z + n) % 4) if c == first else ((y + n) % 4, z)
                    pairs.append(((y * 4 + z) * 2 + c, (to[0] * 4 + to[1]) * 2 + c))
        got.append(lax.ppermute(x, V, pairs))
    return got


def after(x, *others):
    return lax.optimization_barrier((x,) + others)[0]


def per_device(hidden, head_weight, teacher_logits, row_weight):
    pos = jnp.stack([lax.axis_index(a) for a in ("x", "y", "z", "c")]).astype(jnp.int32)
    wt = head_weight.T
    blocks = prep(teacher_logits)
    one = jnp.stack(spread(hidden, 0))
    own = spread(after(one, blocks), 1)
    teacher = lax.all_to_all(after(blocks, *own[1:]), V, 0, 0, tiled=True)
    s, m, l, h, to_right, to_far, to_left = student(pos, wt, own, [swap(x) for x in own])
    t, share = stats(m, l, s, teacher)
    gathered = lax.all_to_all(share, V, 0, 0, tiled=True)

    others = [shift(to_right, 1), shift(to_left, 3), hop(after(hop(to_far), share))]

    w = row_weight.reshape(1, T)
    gu, kl = grad(gathered, after(w, *others), s, t, CUTS[:1])
    gm, gl, _ = grad(gathered, after(w, gu), s, t, CUTS[1:])

    def near(g):
        return [g, shift(g, 1), shift(g, 3)]

    def far(parts):
        half = (parts[0].shape[0] // 2 + 15) // 16 * 16
        return jnp.concatenate([shift(parts[1][:half], 1), shift(parts[2][half:], 3)], axis=0)

    all_u, all_m = lax.all_gather(gu, "x"), lax.all_gather(gm, "x")
    near_l = near(gl)
    far_l = far(near_l)
    mine, other = hidden_part(pos, (gu, gm, gl), wt)
    k = tokens(after(pos, mine), h, [x for other in others for x in (other, swap(other))])
    both = (mine.astype(F32) + swap(after(other, *near_l[1:])).astype(F32)).astype(BF16)
    got = lax.all_to_all(both.reshape(16, T, 128), ("y", "z"), 0, 0, tiled=True)

    head = head_rows(pos, [all_u], k, *CUTS[0])
    head = head_rows(pos, near_l + [far_l], k, *CUTS[2], other=head)
    grad_hidden = jnp.sum(after(got, head).astype(F32), axis=0).astype(BF16)
    head = head_rows(after(pos, grad_hidden), [all_m], k, *CUTS[1], other=head)
    return kl.reshape(T), grad_hidden, head.T


def solution(mesh):
    fine = Mesh(mesh.devices.reshape(4, 4, 4, 2), ("x",) + V)
    in_specs = (P("x", V), P(None, V), P(("x",) + V, None), P("x"))
    out_specs = (P("x"), P("x", V), P("x", V))
    return jax.shard_map(per_device, mesh=fine, in_specs=in_specs, out_specs=out_specs, check_vma=False)
```

```python
import functools

import jax
import jax.numpy as jnp
from jax import lax
from jax.experimental import pallas as pl
from jax.experimental.pallas import tpu as pltpu
from jax.sharding import Mesh
from jax.sharding import PartitionSpec as P

F32, BF16 = jnp.float32, jnp.bfloat16
V = ("y", "z", "c")
NV = 32
VL = 2374
KT = 19
SB = 512
NS = 5
GB = 304
VP = 2432
CUTS = ((0, 4), (4, 1), (5, 3))
T = 512
D = 4096
DX = 1024
LOW = -1e30
MIB = 1 << 20


def call(body, **kw):
    return pl.pallas_call(
        body,
        compiler_params=pltpu.CompilerParams(vmem_limit_bytes=60 * MIB),
        cost_estimate=pl.CostEstimate(flops=1 << 20, bytes_accessed=1 << 16, transcendentals=0),
        **kw,
    )


def whole(shape):
    return pl.BlockSpec(shape, lambda *_: (0,) * len(shape))


def prep_body(t_ref, out_ref):
    end = NV * VL
    for i in range(NV):
        for k in range(KT):
            start = VL * i + 128 * k
            if start + 128 <= end:
                out_ref[i, k] = t_ref[:, start : start + 128]
            else:
                tile = t_ref[:, end - 128 : end].astype(F32)
                out_ref[i, k] = pltpu.roll(tile, end - start, axis=1).astype(BF16)


def prep(teacher):
    shape = (NV, KT, 16, 128)
    return call(
        prep_body,
        out_shape=jax.ShapeDtypeStruct(shape, BF16),
        grid=(1,),
        in_specs=[whole(teacher.shape)],
        out_specs=whole(shape),
    )(teacher)


def fold(x, op):
    return op(x.reshape(-1, 8, T), axis=0)


def student_body(pos, w_ref, *refs):
    own_refs, sib_refs, (s_ref, m_ref, l_ref) = refs[:4], refs[4:8], refs[8:11]
    mine_ref, *next_refs, h_ref = refs[11:]
    step = pl.program_id(0)

    @pl.when(step == 0)
    def _():
        for a in range(4):
            for b in range(4):
                for ref, c in ((own_refs[a], pos[3]), (sib_refs[a], 1 - pos[3])):
                    y = (pos[1] + 4 - jnp.where(c == 0, a, b)) % 4
                    z = (pos[2] + 4 - jnp.where(c == 0, b, a)) % 4
                    at = pl.multiple_of(((y * 4 + z) * 2 + c) * 128, 128)
                    h_ref[:, pl.ds(at, 128)] = ref[b]
        mine_ref[...] = h_ref[:, pl.ds(pl.multiple_of(pos[0] * DX, 128), DX)]
        for n, out_ref in enumerate(next_refs, 1):
            for z in range(4):
                at = pl.multiple_of((pos[0] + n) % 4 * DX + (2 * z + pos[3]) * 128, 128)
                out_ref[z] = h_ref[:, pl.ds(at, 128)]
        m_ref[...] = jnp.full_like(m_ref, LOW)
        l_ref[...] = jnp.zeros_like(l_ref)

    s = lax.dot_general(w_ref[...], h_ref[...], (((1,), (1,)), ((), ())), preferred_element_type=F32)
    rows = step * SB + lax.broadcasted_iota(jnp.int32, s.shape, 0)
    s = jnp.where(rows < VL, s, LOW)
    s_ref[...] = s
    old = m_ref[...]
    peak = jnp.maximum(old, fold(s, jnp.max))
    m_ref[...] = peak
    es = jnp.exp(s.reshape(-1, 8, T) - peak[None])
    l_ref[...] = l_ref[...] * jnp.exp(old - peak) + jnp.sum(es, axis=0)


def student(pos, wt, own, sib):
    part = jax.ShapeDtypeStruct((8, T), F32)
    return call(
        student_body,
        out_shape=[
            jax.ShapeDtypeStruct((NS * SB, T), F32),
            part,
            part,
            jax.ShapeDtypeStruct((T, DX), BF16),
            *[jax.ShapeDtypeStruct((4, T, 128), BF16)] * 3,
        ],
        grid_spec=pltpu.PrefetchScalarGridSpec(
            num_scalar_prefetch=1,
            grid=(NS,),
            in_specs=[pl.BlockSpec((SB, D), lambda i, p: (i, 0))] + [whole((4, T, 128))] * 8,
            out_specs=[
                pl.BlockSpec((SB, T), lambda i, p: (i, 0)),
                whole((8, T)),
                whole((8, T)),
                whole((T, DX)),
                *[whole((4, T, 128))] * 3,
            ],
            scratch_shapes=[pltpu.VMEM((T, D), BF16)],
        ),
    )(pos, wt, *own, *sib)


def stats_body(m_ref, l_ref, s_ref, t_ref, tt_ref, out_ref, p_ref, sum_ref, cross_ref):
    step = pl.program_id(0)

    @pl.when(step == 0)
    def _():
        p_ref[...] = jnp.full_like(p_ref, LOW)
        sum_ref[...] = jnp.zeros_like(sum_ref)
        cross_ref[...] = jnp.zeros_like(cross_ref)

    for n in range(SB // 128):

        @pl.when(step * (SB // 128) + n < KT)
        def _():
            t = t_ref[:, n].reshape(T, 128).T.astype(F32)
            rows = step * SB + n * 128 + lax.broadcasted_iota(jnp.int32, t.shape, 0)
            t = jnp.where(rows < VL, t, LOW)
            tt_ref[n * 128 : (n + 1) * 128, :] = t.astype(BF16)
            old = p_ref[...]
            peak = jnp.maximum(old, fold(t, jnp.max))
            p_ref[...] = peak
            scale = jnp.exp(old - peak)
            t = t.reshape(-1, 8, T)
            et = jnp.exp(t - peak[None])
            s = s_ref[n * 128 : (n + 1) * 128, :].reshape(-1, 8, T)
            sum_ref[...] = sum_ref[...] * scale + jnp.sum(et, axis=0)
            cross_ref[...] = cross_ref[...] * scale + jnp.sum(et * (t - s), axis=0)

    @pl.when(step == NS - 1)
    def _():
        s_peak = jnp.max(m_ref[...], axis=0, keepdims=True)
        t_peak = jnp.max(p_ref[...], axis=0, keepdims=True)
        se, te = jnp.exp(m_ref[...] - s_peak), jnp.exp(p_ref[...] - t_peak)
        total = lambda scale, ref: jnp.sum(scale * ref[...], axis=0, keepdims=True)
        values = [s_peak, t_peak, total(se, l_ref), total(te, sum_ref), total(te, cross_ref)]
        row = lax.broadcasted_iota(jnp.int32, (8, T), 0)
        out = jnp.zeros((8, T), F32)
        for n, v in enumerate(values):
            out = jnp.where(row == n, v, out)
        for i in range(NV):
            out_ref[i] = out


def stats(m, l, s, t):
    block = pl.BlockSpec((SB, T), lambda i: (i, 0))
    return call(
        stats_body,
        out_shape=[jax.ShapeDtypeStruct((NS * SB, T), BF16), jax.ShapeDtypeStruct((NV, 8, T), F32)],
        grid=(NS,),
        in_specs=[
            whole((8, T)),
            whole((8, T)),
            block,
            pl.BlockSpec((NV, SB // 128, 16, 128), lambda i: (0, i, 0, 0)),
        ],
        out_specs=[block, whole((NV, 8, T))],
        scratch_shapes=[pltpu.VMEM((8, T), F32)] * 3,
    )(m, l, s, t)


def grad_body(cuts, all_ref, w_ref, s_ref, t_ref, *refs):
    kl_ref, c_ref = refs[-2:]
    step = pl.program_id(0)

    @pl.when(step == 0)
    def _():
        v = all_ref[...]
        s_peak, t_peak = jnp.max(v[:, 0:1, :], axis=0), jnp.max(v[:, 1:2, :], axis=0)
        se, te = jnp.exp(v[:, 0:1, :] - s_peak[None]), jnp.exp(v[:, 1:2, :] - t_peak[None])
        total = lambda scale, n: jnp.sum(scale * v[:, n : n + 1, :], axis=0)
        s_tot, t_tot, cross = total(se, 2), total(te, 3), total(te, 4)
        kl_ref[...] = cross / t_tot - t_peak - jnp.log(t_tot) + s_peak + jnp.log(s_tot)
        c_ref[0:1, :] = s_peak
        c_ref[1:2, :] = t_peak
        c_ref[2:3, :] = w_ref[...] / s_tot
        c_ref[3:4, :] = w_ref[...] / t_tot

    es = jnp.exp(s_ref[...] - c_ref[0:1, :]) * c_ref[2:3, :]
    et = jnp.exp(t_ref[...].astype(F32) - c_ref[1:2, :]) * c_ref[3:4, :]
    g = (es - et).astype(BF16)
    at = step + cuts[0][0]
    for (first, steps), g_ref in zip(cuts, refs):

        @pl.when((at >= first) & (at < first + steps))
        def _():
            g_ref[...] = g


def piece(start, first, steps):
    return pl.BlockSpec((GB, T), lambda i: (jnp.clip(i + start - first, 0, steps - 1), 0))


def grad(gathered, w, s, t, cuts):
    start = cuts[0][0]
    block = pl.BlockSpec((GB, T), lambda i: (i + start, 0))
    return call(
        functools.partial(grad_body, cuts),
        out_shape=[jax.ShapeDtypeStruct((n * GB, T), BF16) for _, n in cuts] + [jax.ShapeDtypeStruct((1, T), F32)],
        grid=(sum(n for _, n in cuts),),
        in_specs=[whole((NV, 8, T)), whole((1, T)), block, block],
        out_specs=[piece(start, *cut) for cut in cuts] + [whole((1, T))],
        scratch_shapes=[pltpu.VMEM((8, T), F32)],
    )(gathered, w, s, t)


def hidden_body(pos, *refs):
    g_refs, (w_ref, mine_ref, other_ref, gt_ref) = refs[: len(CUTS)], refs[len(CUTS) :]

    @pl.when(pl.program_id(0) == 0)
    def _():
        for lo in range(0, VP, 128):
            rows = []
            for (first, steps), ref in zip(CUTS, g_refs):
                start, end = max(lo - first * GB, 0), min(lo + 128 - first * GB, steps * GB)
                if start < end:
                    rows.append(ref[start:end, :])
            x = jnp.concatenate(rows, axis=0)
            gt_ref[:, lo : lo + 128] = x.astype(F32).T.astype(BF16)

    p = jnp.dot(gt_ref[:, :VL], w_ref[...], preferred_element_type=F32).astype(BF16)
    even = pos[3] == 0
    for z in range(4):
        first, second = p[:, 256 * z : 256 * z + 128], p[:, 256 * z + 128 : 256 * z + 256]
        mine_ref[0, z] = jnp.where(even, first, second)
        other_ref[0, z] = jnp.where(even, second, first)


def hidden_part(pos, gs, wt):
    out = pl.BlockSpec((1, 4, T, 128), lambda i, p: (i, 0, 0, 0))
    return call(
        hidden_body,
        out_shape=[jax.ShapeDtypeStruct((4, 4, T, 128), BF16)] * 2,
        grid_spec=pltpu.PrefetchScalarGridSpec(
            num_scalar_prefetch=1,
            grid=(4,),
            in_specs=[whole(g.shape) for g in gs] + [pl.BlockSpec((VL, 1024), lambda i, p: (0, i))],
            out_specs=[out, out],
            scratch_shapes=[pltpu.VMEM((T, VP), BF16)],
        ),
    )(pos, *gs, wt)


def tokens_body(pos, h_ref, *refs):
    k_ref = refs[-1]
    k_ref[0:T, :] = h_ref[...]
    for n in range(3):
        rows = slice((n + 1) * T, (n + 2) * T)
        for ref, c in ((refs[2 * n], pos[3]), (refs[2 * n + 1], 1 - pos[3])):
            for z in range(4):
                k_ref[rows, pl.ds(pl.multiple_of((2 * z + c) * 128, 128), 128)] = ref[z]


def tokens(pos, h, parts):
    return call(
        tokens_body,
        out_shape=jax.ShapeDtypeStruct((4 * T, DX), BF16),
        grid_spec=pltpu.PrefetchScalarGridSpec(
            num_scalar_prefetch=1,
            grid=(1,),
            in_specs=[whole((T, DX))] + [whole((4, T, 128))] * 6,
            out_specs=whole((4 * T, DX)),
        ),
    )(pos, h, *parts)


def head_body(pos, *refs):
    g = jnp.concatenate([r[...].reshape(-1, T) for r in refs[:4]], axis=1)
    refs[-1][...] = jnp.dot(g, refs[4][...], preferred_element_type=F32).astype(BF16)


def head_rows(pos, gs, k, first, steps, other=None):
    if len(gs) == 1:
        rows = GB * 2 if steps % 2 == 0 else GB
        specs = [
            pl.BlockSpec((1, rows, T), functools.partial(lambda away, i, p: ((p[0] + away) % 4, i, 0), away))
            for away in (0, 3, 1, 2)
        ]
    else:
        rows = GB
        specs = [pl.BlockSpec((rows, T), lambda i, p: (i, 0))] * 4
    start = first * GB // rows
    specs.append(whole((4 * T, DX)))
    args = [*(gs * 4 if len(gs) == 1 else gs), k]
    kw = {}
    if other is not None:
        specs.append(pl.BlockSpec(memory_space=pl.ANY))
        args.append(other)
        kw["input_output_aliases"] = {len(args): 0}
    return call(
        head_body,
        out_shape=jax.ShapeDtypeStruct((VL, DX), BF16),
        grid_spec=pltpu.PrefetchScalarGridSpec(
            num_scalar_prefetch=1,
            grid=(steps * GB // rows,),
            in_specs=specs,
            out_specs=pl.BlockSpec((rows, DX), lambda i, p: (i + start, 0)),
        ),
        **kw,
    )(pos, *args)


def shift(x, n):
    return lax.ppermute(x, "x", [(i, (i + n) % 4) for i in range(4)])


def hop(x):
    return lax.ppermute(x, ("x", "c"), [(2 * i + c, (i + 1 + 2 * c) % 4 * 2 + c) for i in range(4) for c in range(2)])


def swap(x):
    return lax.ppermute(x, "c", [(0, 1), (1, 0)])


def spread(x, first):
    got = [x]
    for n in (1, 2, 3):
        pairs = []
        for y in range(4):
            for z in range(4):
                for c in range(2):
                    to = (y, (z + n) % 4) if c == first else ((y + n) % 4, z)
                    pairs.append(((y * 4 + z) * 2 + c, (to[0] * 4 + to[1]) * 2 + c))
        got.append(lax.ppermute(x, V, pairs))
    return got


def after(x, *others):
    return lax.optimization_barrier((x,) + others)[0]


def per_device(hidden, head_weight, teacher_logits, row_weight):
    pos = jnp.stack([lax.axis_index(a) for a in ("x", "y", "z", "c")]).astype(jnp.int32)
    wt = head_weight.T
    blocks = prep(teacher_logits)
    one = jnp.stack(spread(hidden, 0))
    own = spread(after(one, blocks), 1)
    teacher = lax.all_to_all(after(blocks, *own[1:]), V, 0, 0, tiled=True)
    s, m, l, h, to_right, to_far, to_left = student(pos, wt, own, [swap(x) for x in own])
    t, share = stats(m, l, s, teacher)
    gathered = lax.all_to_all(share, V, 0, 0, tiled=True)

    others = [shift(to_right, 1), shift(to_left, 3), hop(after(hop(to_far), share))]

    w = row_weight.reshape(1, T)
    gu, kl = grad(gathered, after(w, *others), s, t, CUTS[:1])
    gm, gl, _ = grad(gathered, after(w, gu), s, t, CUTS[1:])

    def near(g):
        return [g, shift(g, 1), shift(g, 3)]

    def far(parts):
        half = (parts[0].shape[0] // 2 + 15) // 16 * 16
        return [shift(parts[1][:half], 1), shift(parts[2][half:], 3)]

    all_u, all_m = lax.all_gather(gu, "x"), lax.all_gather(gm, "x")
    near_l = near(gl)
    far_l = far(near_l)
    mine, other = hidden_part(pos, (gu, gm, gl), wt)
    others = [x for other in others for x in (other, swap(after(other, gathered)))]
    k = tokens(after(pos, mine), h, others)
    both = (mine.astype(F32) + swap(after(other, k, *near_l[1:])).astype(F32)).astype(BF16)
    got = lax.all_to_all(both.reshape(16, T, 128), ("y", "z"), 0, 0, tiled=True)

    head = head_rows(pos, [all_u], k, *CUTS[0])
    far_l = jnp.concatenate([after(x, head) for x in far_l], axis=0)
    head = head_rows(pos, near_l + [far_l], k, *CUTS[2], other=head)
    grad_hidden = jnp.sum(after(got, head).astype(F32), axis=0).astype(BF16)
    head = head_rows(after(pos, grad_hidden), [all_m], k, *CUTS[1], other=head)
    return kl.reshape(T), grad_hidden, head.T


def solution(mesh):
    fine = Mesh(mesh.devices.reshape(4, 4, 4, 2), ("x",) + V)
    in_specs = (P("x", V), P(None, V), P(("x",) + V, None), P("x"))
    out_specs = (P("x"), P("x", V), P("x", V))
    return jax.shard_map(per_device, mesh=fine, in_specs=in_specs, out_specs=out_specs, check_vma=False)
```

```python
import functools

import jax
import jax.numpy as jnp
from jax import lax
from jax.experimental import pallas as pl
from jax.experimental.pallas import tpu as pltpu
from jax.sharding import Mesh
from jax.sharding import PartitionSpec as P

F32, BF16 = jnp.float32, jnp.bfloat16
V = ("y", "z", "c")
NV = 32
VL = 2374
KT = 19
SB = 512
NS = 5
GB = 304
VP = 2432
CUTS = ((0, 4), (4, 1), (5, 3))
T = 512
D = 4096
DX = 1024
LOW = -1e30
MIB = 1 << 20


def call(body, **kw):
    return pl.pallas_call(
        body,
        compiler_params=pltpu.CompilerParams(vmem_limit_bytes=60 * MIB),
        cost_estimate=pl.CostEstimate(flops=1 << 20, bytes_accessed=1 << 16, transcendentals=0),
        **kw,
    )


def whole(shape):
    return pl.BlockSpec(shape, lambda *_: (0,) * len(shape))


def prep_body(t_ref, out_ref):
    end = NV * VL
    for i in range(NV):
        for k in range(KT):
            start = VL * i + 128 * k
            if start + 128 <= end:
                out_ref[i, k] = t_ref[:, start : start + 128]
            else:
                tile = t_ref[:, end - 128 : end].astype(F32)
                out_ref[i, k] = pltpu.roll(tile, end - start, axis=1).astype(BF16)


def prep(teacher):
    shape = (NV, KT, 16, 128)
    return call(
        prep_body,
        out_shape=jax.ShapeDtypeStruct(shape, BF16),
        grid=(1,),
        in_specs=[whole(teacher.shape)],
        out_specs=whole(shape),
    )(teacher)


def fold(x, op):
    return op(x.reshape(-1, 8, T), axis=0)


def student_body(pos, w_ref, *refs):
    own_refs, sib_refs, (s_ref, m_ref, l_ref) = refs[:4], refs[4:8], refs[8:11]
    mine_ref, *next_refs, h_ref = refs[11:]
    step = pl.program_id(0)

    @pl.when(step == 0)
    def _():
        for a in range(4):
            for b in range(4):
                for ref, c in ((own_refs[a], pos[3]), (sib_refs[a], 1 - pos[3])):
                    y = (pos[1] + 4 - jnp.where(c == 0, a, b)) % 4
                    z = (pos[2] + 4 - jnp.where(c == 0, b, a)) % 4
                    at = pl.multiple_of(((y * 4 + z) * 2 + c) * 128, 128)
                    h_ref[:, pl.ds(at, 128)] = ref[b]
        mine_ref[...] = h_ref[:, pl.ds(pl.multiple_of(pos[0] * DX, 128), DX)]
        for n, out_ref in enumerate(next_refs, 1):
            for z in range(4):
                at = pl.multiple_of((pos[0] + n) % 4 * DX + (2 * z + pos[3]) * 128, 128)
                out_ref[z] = h_ref[:, pl.ds(at, 128)]
        m_ref[...] = jnp.full_like(m_ref, LOW)
        l_ref[...] = jnp.zeros_like(l_ref)

    s = lax.dot_general(w_ref[...], h_ref[...], (((1,), (1,)), ((), ())), preferred_element_type=F32)
    rows = step * SB + lax.broadcasted_iota(jnp.int32, s.shape, 0)
    s = jnp.where(rows < VL, s, LOW)
    s_ref[...] = s
    old = m_ref[...]
    peak = jnp.maximum(old, fold(s, jnp.max))
    m_ref[...] = peak
    es = jnp.exp(s.reshape(-1, 8, T) - peak[None])
    l_ref[...] = l_ref[...] * jnp.exp(old - peak) + jnp.sum(es, axis=0)


def student(pos, wt, own, sib):
    part = jax.ShapeDtypeStruct((8, T), F32)
    return call(
        student_body,
        out_shape=[
            jax.ShapeDtypeStruct((NS * SB, T), F32),
            part,
            part,
            jax.ShapeDtypeStruct((T, DX), BF16),
            *[jax.ShapeDtypeStruct((4, T, 128), BF16)] * 3,
        ],
        grid_spec=pltpu.PrefetchScalarGridSpec(
            num_scalar_prefetch=1,
            grid=(NS,),
            in_specs=[pl.BlockSpec((SB, D), lambda i, p: (i, 0))] + [whole((4, T, 128))] * 8,
            out_specs=[
                pl.BlockSpec((SB, T), lambda i, p: (i, 0)),
                whole((8, T)),
                whole((8, T)),
                whole((T, DX)),
                *[whole((4, T, 128))] * 3,
            ],
            scratch_shapes=[pltpu.VMEM((T, D), BF16)],
        ),
    )(pos, wt, *own, *sib)


def stats_body(m_ref, l_ref, s_ref, t_ref, tt_ref, out_ref, p_ref, sum_ref, cross_ref):
    step = pl.program_id(0)

    @pl.when(step == 0)
    def _():
        p_ref[...] = jnp.full_like(p_ref, LOW)
        sum_ref[...] = jnp.zeros_like(sum_ref)
        cross_ref[...] = jnp.zeros_like(cross_ref)

    for n in range(SB // 128):

        @pl.when(step * (SB // 128) + n < KT)
        def _():
            t = t_ref[:, n].reshape(T, 128).T.astype(F32)
            rows = step * SB + n * 128 + lax.broadcasted_iota(jnp.int32, t.shape, 0)
            t = jnp.where(rows < VL, t, LOW)
            tt_ref[n * 128 : (n + 1) * 128, :] = t.astype(BF16)
            old = p_ref[...]
            peak = jnp.maximum(old, fold(t, jnp.max))
            p_ref[...] = peak
            scale = jnp.exp(old - peak)
            t = t.reshape(-1, 8, T)
            et = jnp.exp(t - peak[None])
            s = s_ref[n * 128 : (n + 1) * 128, :].reshape(-1, 8, T)
            sum_ref[...] = sum_ref[...] * scale + jnp.sum(et, axis=0)
            cross_ref[...] = cross_ref[...] * scale + jnp.sum(et * (t - s), axis=0)

    @pl.when(step == NS - 1)
    def _():
        s_peak = jnp.max(m_ref[...], axis=0, keepdims=True)
        t_peak = jnp.max(p_ref[...], axis=0, keepdims=True)
        se, te = jnp.exp(m_ref[...] - s_peak), jnp.exp(p_ref[...] - t_peak)
        total = lambda scale, ref: jnp.sum(scale * ref[...], axis=0, keepdims=True)
        values = [s_peak, t_peak, total(se, l_ref), total(te, sum_ref), total(te, cross_ref)]
        row = lax.broadcasted_iota(jnp.int32, (8, T), 0)
        out = jnp.zeros((8, T), F32)
        for n, v in enumerate(values):
            out = jnp.where(row == n, v, out)
        for i in range(NV):
            out_ref[i] = out


def stats(m, l, s, t):
    block = pl.BlockSpec((SB, T), lambda i: (i, 0))
    return call(
        stats_body,
        out_shape=[jax.ShapeDtypeStruct((NS * SB, T), BF16), jax.ShapeDtypeStruct((NV, 8, T), F32)],
        grid=(NS,),
        in_specs=[
            whole((8, T)),
            whole((8, T)),
            block,
            pl.BlockSpec((NV, SB // 128, 16, 128), lambda i: (0, i, 0, 0)),
        ],
        out_specs=[block, whole((NV, 8, T))],
        scratch_shapes=[pltpu.VMEM((8, T), F32)] * 3,
    )(m, l, s, t)


def grad_body(cuts, all_ref, w_ref, s_ref, t_ref, *refs):
    kl_ref, c_ref = refs[-2:]
    step = pl.program_id(0)

    @pl.when(step == 0)
    def _():
        v = all_ref[...]
        s_peak, t_peak = jnp.max(v[:, 0:1, :], axis=0), jnp.max(v[:, 1:2, :], axis=0)
        se, te = jnp.exp(v[:, 0:1, :] - s_peak[None]), jnp.exp(v[:, 1:2, :] - t_peak[None])
        total = lambda scale, n: jnp.sum(scale * v[:, n : n + 1, :], axis=0)
        s_tot, t_tot, cross = total(se, 2), total(te, 3), total(te, 4)
        kl_ref[...] = cross / t_tot - t_peak - jnp.log(t_tot) + s_peak + jnp.log(s_tot)
        c_ref[0:1, :] = s_peak
        c_ref[1:2, :] = t_peak
        c_ref[2:3, :] = w_ref[...] / s_tot
        c_ref[3:4, :] = w_ref[...] / t_tot

    es = jnp.exp(s_ref[...] - c_ref[0:1, :]) * c_ref[2:3, :]
    et = jnp.exp(t_ref[...].astype(F32) - c_ref[1:2, :]) * c_ref[3:4, :]
    g = (es - et).astype(BF16)
    at = step + cuts[0][0]
    for (first, steps), g_ref in zip(cuts, refs):

        @pl.when((at >= first) & (at < first + steps))
        def _():
            g_ref[...] = g


def piece(start, first, steps):
    return pl.BlockSpec((GB, T), lambda i: (jnp.clip(i + start - first, 0, steps - 1), 0))


def grad(gathered, w, s, t, cuts):
    start = cuts[0][0]
    block = pl.BlockSpec((GB, T), lambda i: (i + start, 0))
    return call(
        functools.partial(grad_body, cuts),
        out_shape=[jax.ShapeDtypeStruct((n * GB, T), BF16) for _, n in cuts] + [jax.ShapeDtypeStruct((1, T), F32)],
        grid=(sum(n for _, n in cuts),),
        in_specs=[whole((NV, 8, T)), whole((1, T)), block, block],
        out_specs=[piece(start, *cut) for cut in cuts] + [whole((1, T))],
        scratch_shapes=[pltpu.VMEM((8, T), F32)],
    )(gathered, w, s, t)


def hidden_body(pos, *refs):
    g_refs, (w_ref, mine_ref, other_ref, gt_ref) = refs[: len(CUTS)], refs[len(CUTS) :]

    @pl.when(pl.program_id(0) == 0)
    def _():
        for lo in range(0, VP, 128):
            rows = []
            for (first, steps), ref in zip(CUTS, g_refs):
                start, end = max(lo - first * GB, 0), min(lo + 128 - first * GB, steps * GB)
                if start < end:
                    rows.append(ref[start:end, :])
            x = jnp.concatenate(rows, axis=0)
            gt_ref[:, lo : lo + 128] = x.astype(F32).T.astype(BF16)

    p = jnp.dot(gt_ref[:, :VL], w_ref[...], preferred_element_type=F32).astype(BF16)
    even = pos[3] == 0
    for z in range(4):
        first, second = p[:, 256 * z : 256 * z + 128], p[:, 256 * z + 128 : 256 * z + 256]
        mine_ref[0, z] = jnp.where(even, first, second)
        other_ref[0, z] = jnp.where(even, second, first)


def hidden_part(pos, gs, wt):
    out = pl.BlockSpec((1, 4, T, 128), lambda i, p: (i, 0, 0, 0))
    return call(
        hidden_body,
        out_shape=[jax.ShapeDtypeStruct((4, 4, T, 128), BF16)] * 2,
        grid_spec=pltpu.PrefetchScalarGridSpec(
            num_scalar_prefetch=1,
            grid=(4,),
            in_specs=[whole(g.shape) for g in gs] + [pl.BlockSpec((VL, 1024), lambda i, p: (0, i))],
            out_specs=[out, out],
            scratch_shapes=[pltpu.VMEM((T, VP), BF16)],
        ),
    )(pos, *gs, wt)


def tokens_body(pos, h_ref, *refs):
    k_ref = refs[-1]
    k_ref[0:T, :] = h_ref[...]
    for n in range(3):
        rows = slice((n + 1) * T, (n + 2) * T)
        for ref, c in ((refs[2 * n], pos[3]), (refs[2 * n + 1], 1 - pos[3])):
            for z in range(4):
                k_ref[rows, pl.ds(pl.multiple_of((2 * z + c) * 128, 128), 128)] = ref[z]


def tokens(pos, h, parts):
    return call(
        tokens_body,
        out_shape=jax.ShapeDtypeStruct((4 * T, DX), BF16),
        grid_spec=pltpu.PrefetchScalarGridSpec(
            num_scalar_prefetch=1,
            grid=(1,),
            in_specs=[whole((T, DX))] + [whole((4, T, 128))] * 6,
            out_specs=whole((4 * T, DX)),
        ),
    )(pos, h, *parts)


def head_body(pos, *refs):
    g = jnp.concatenate([r[...].reshape(-1, T) for r in refs[:4]], axis=1)
    refs[-1][...] = jnp.dot(g, refs[4][...], preferred_element_type=F32).astype(BF16)


def head_rows(pos, gs, k, first, steps, other=None):
    if len(gs) == 1:
        rows = GB * 2 if steps % 2 == 0 else GB
        specs = [
            pl.BlockSpec((1, rows, T), functools.partial(lambda away, i, p: ((p[0] + away) % 4, i, 0), away))
            for away in (0, 3, 1, 2)
        ]
    else:
        rows = GB
        specs = [pl.BlockSpec((rows, T), lambda i, p: (i, 0))] * 4
    start = first * GB // rows
    specs.append(whole((4 * T, DX)))
    args = [*(gs * 4 if len(gs) == 1 else gs), k]
    kw = {}
    if other is not None:
        specs.append(pl.BlockSpec(memory_space=pl.ANY))
        args.append(other)
        kw["input_output_aliases"] = {len(args): 0}
    return call(
        head_body,
        out_shape=jax.ShapeDtypeStruct((VL, DX), BF16),
        grid_spec=pltpu.PrefetchScalarGridSpec(
            num_scalar_prefetch=1,
            grid=(steps * GB // rows,),
            in_specs=specs,
            out_specs=pl.BlockSpec((rows, DX), lambda i, p: (i + start, 0)),
        ),
        **kw,
    )(pos, *args)


def shift(x, n):
    return lax.ppermute(x, "x", [(i, (i + n) % 4) for i in range(4)])


def hop(x):
    return lax.ppermute(x, ("x", "c"), [(2 * i + c, (i + 1 + 2 * c) % 4 * 2 + c) for i in range(4) for c in range(2)])


def swap(x):
    return lax.ppermute(x, "c", [(0, 1), (1, 0)])


def spread(x, first):
    got = [x]
    for n in (1, 2, 3):
        pairs = []
        for y in range(4):
            for z in range(4):
                for c in range(2):
                    to = (y, (z + n) % 4) if c == first else ((y + n) % 4, z)
                    pairs.append(((y * 4 + z) * 2 + c, (to[0] * 4 + to[1]) * 2 + c))
        got.append(lax.ppermute(x, V, pairs))
    return got


def after(x, *others):
    return lax.optimization_barrier((x,) + others)[0]


def per_device(hidden, head_weight, teacher_logits, row_weight):
    pos = jnp.stack([lax.axis_index(a) for a in ("x", "y", "z", "c")]).astype(jnp.int32)
    wt = head_weight.T
    blocks = prep(teacher_logits)
    one = jnp.stack(spread(hidden, 0))
    own = spread(after(one, blocks), 1)
    teacher = lax.all_to_all(after(blocks, *own[1:]), V, 0, 0, tiled=True)
    s, m, l, h, to_right, to_far, to_left = student(pos, wt, own, [swap(x) for x in own])
    t, share = stats(m, l, s, teacher)
    gathered = lax.all_to_all(share, V, 0, 0, tiled=True)

    others = [shift(to_right, 1), shift(to_left, 3), hop(after(hop(to_far), share))]

    w = row_weight.reshape(1, T)
    gu, kl = grad(gathered, after(w, *others), s, t, CUTS[:1])
    gm, gl, _ = grad(gathered, after(w, gu), s, t, CUTS[1:])

    def near(g):
        return [g, shift(g, 1), shift(g, 3)]

    def far(parts):
        half = (parts[0].shape[0] // 2 + 15) // 16 * 16
        return [shift(parts[1][:half], 1), shift(parts[2][half:], 3)]

    all_u, all_m = lax.all_gather(gu, "x"), lax.all_gather(gm, "x")
    near_l = near(gl)
    far_l = far(near_l)
    mine, other = hidden_part(pos, (gu, gm, gl), wt)
    others = [x for other in others for x in (other, swap(after(other, gathered)))]
    k = tokens(after(pos, mine), h, others)
    both = (mine.astype(F32) + swap(after(other, k)).astype(F32)).astype(BF16)
    got = lax.all_to_all(both.reshape(16, T, 128), ("y", "z"), 0, 0, tiled=True)

    head = head_rows(pos, [all_u], k, *CUTS[0])
    far_l = jnp.concatenate([after(x, head) for x in far_l], axis=0)
    head = head_rows(pos, near_l + [far_l], k, *CUTS[2], other=head)
    grad_hidden = jnp.sum(after(got, head).astype(F32), axis=0).astype(BF16)
    head = head_rows(after(pos, grad_hidden), [all_m], k, *CUTS[1], other=head)
    return kl.reshape(T), grad_hidden, head.T


def solution(mesh):
    fine = Mesh(mesh.devices.reshape(4, 4, 4, 2), ("x",) + V)
    in_specs = (P("x", V), P(None, V), P(("x",) + V, None), P("x"))
    out_specs = (P("x"), P("x", V), P("x", V))
    return jax.shard_map(per_device, mesh=fine, in_specs=in_specs, out_specs=out_specs, check_vma=False)
```
